512 devices in a mesh: grp: 16 (over z_hi, x), blk: 32 (over z_lo, y, core).
Axes of the slice: x: 4, y: 8, z: 8 (z_hi: 4, z_lo: 2; z = z_hi * 2 + z_lo), core: 2. Of those that a mesh axis runs over, the one named last changes fastest.
Arguments:
- src_embed: bfloat16 [262144, 256], P(('grp', 'blk')), may hold values from -1.5 to 1.5
- dst_embed: bfloat16 [262144, 256], P(('grp', 'blk')), may hold values from -1.5 to 1.5
- relation: float32 [1345, 256], replicated, may hold values from 0.1 to 1.9
- src_index: int32 [16, 32, 4, 512], P('grp', 'blk'), may hold values from 0 to 511
- dst_index: int32 [16, 32, 4, 512], P('grp', 'blk'), may hold values from 0 to 511
- rel_index: int32 [16, 32, 4, 512], P('grp', 'blk'), may hold values from 0 to 1344
- neg_index: int32 [16, 32, 4, 512], P('grp', 'blk'), may hold values from 0 to 511
- edge_count: int32 [16, 32, 4], P('grp', 'blk'), may hold values from 1 to 512, 1024 in all within a row
Outputs:
- grad_src: float32 [262144, 256], P(('grp', 'blk'))
- grad_dst: float32 [262144, 256], P(('grp', 'blk'))
- grad_rel: float32 [1345, 256], replicated
The draws below stay inside these ranges and needn't reach their ends.
Inputs may be any that keep to these rules, and one draw needn't show every extreme that they name: `edge_count`: within one device's tiles the counts sum to 1024, and one tile of each device is full.
All inputs are finite; a program needn't handle non-finite values.
Results may differ from the reference program's by a relative error of at most 0.004.
Values may be sent and summed in bfloat16 or wider, within the bound.
A program may use at most 64 MiB of HBM per device.

```python
import math
import jax
import jax.numpy as jnp
import numpy as np
from jax import lax

D = 256
RELS = 1345
E_DEV = 512
EDGE_CAP = 512
NEG = 512
STEPS = 4
GROUPS = 16
BLOCKS = 32
ENTITIES = 262144


def plant(result, key, least, high):
    shape = result.shape
    place = [jax.random.randint(jax.random.fold_in(key, axis), (), 0, shape[axis]) for axis in range(len(shape))]
    result = result.at[tuple(place)].set(least)
    longest = shape.index(max(shape))
    place[longest] = (place[longest] + 1) % shape[longest]
    return result.at[tuple(place)].set(high)


def shard_levels(own_key, extent, pieces, smallest, largest):
    factor_of, own = 1.0, jax.random.fold_in(own_key, 6)
    for axis_at, blocks in pieces:
        steps = jnp.exp(jax.random.uniform(jax.random.fold_in(own, axis_at), (blocks,), jnp.float32, smallest / len(pieces), largest / len(pieces)))
        factor_of = factor_of * jnp.repeat(steps, extent[axis_at] // blocks).reshape([-1 if axis == axis_at else 1 for axis in range(len(extent))])
    return factor_of


def length_profile(amount, total, reach, skew):
    loads = [(1 << 20) // math.isqrt(rank ** skew) + 1 for rank in range(2, amount + 1)]
    rest, counts = total - reach - (amount - 1), [1] * (amount - 1)
    while rest > 0:
        free = [i for i in range(amount - 1) if counts[i] < reach]
        mass, left = sum([loads[i] for i in free]), rest
        for i in free:
            addition = min(reach - counts[i], max(1, left * loads[i] // mass), rest)
            counts[i] = counts[i] + addition
            rest = rest - addition
    return np.array([reach] + counts)


def ragged(own_key, count, total, most, lean):
    if count == 2:
        one = jax.random.randint(own_key, (), max(1, total - most), min(most, total - 1) + 1)
        return jnp.stack([one, total - one])
    tallies = jnp.asarray(length_profile(count, total, most, lean), jnp.int32)
    couples = (count - 1) // 2
    source_of, receiver = tallies[1:1 + 2 * couples:2], tallies[2:2 + 2 * couples:2]
    margin = jnp.minimum(source_of - 1, most - receiver)
    moved = jax.random.randint(jax.random.fold_in(own_key, 1), (couples,), 0, 1 << 20) % (margin + 1)
    tallies = tallies.at[1:1 + 2 * couples:2].set(source_of - moved).at[2:2 + 2 * couples:2].set(receiver + moved)
    return tallies[jax.random.permutation(jax.random.fold_in(own_key, 2), count)]


def gaussian(key, extent, spread, bound, pieces=(), kind=jnp.bfloat16):
    entries = jax.random.normal(key, extent, jnp.float32) * spread
    if len(pieces) > 0:
        entries = shard_levels(key, extent, pieces, -0.22, 0.18) * entries
    return jnp.clip(entries, min=-bound, max=bound).astype(kind)


def setup_inputs(seed: int = 0) -> dict:
    arg_keys = jax.random.split(jax.random.key(seed), 9)
    src_embed = gaussian(arg_keys[0], (ENTITIES, D), 0.25, 1.5, ((0, 512),))
    dst_embed = gaussian(arg_keys[1], (ENTITIES, D), 0.25, 1.5, ((0, 512),))
    relation = jnp.clip(1.0 + 0.18 * jax.random.normal(arg_keys[2], (RELS, D), jnp.float32), 0.1, 1.9)
    src_index = plant(jax.random.randint(arg_keys[3], (GROUPS, BLOCKS, STEPS, EDGE_CAP), 0, E_DEV), jax.random.fold_in(arg_keys[3], 1), 0, E_DEV - 1).astype(jnp.int32)
    dst_index = plant(jax.random.randint(arg_keys[4], (GROUPS, BLOCKS, STEPS, EDGE_CAP), 0, E_DEV), jax.random.fold_in(arg_keys[4], 1), 0, E_DEV - 1).astype(jnp.int32)
    rel_index = plant(jax.random.randint(arg_keys[5], (GROUPS, BLOCKS, STEPS, EDGE_CAP), 0, RELS), jax.random.fold_in(arg_keys[5], 1), 0, RELS - 1).astype(jnp.int32)
    neg_index = plant(jax.random.randint(arg_keys[6], (GROUPS, BLOCKS, STEPS, NEG), 0, E_DEV), jax.random.fold_in(arg_keys[6], 1), 0, E_DEV - 1).astype(jnp.int32)
    edge_count = jax.vmap(lambda own: ragged(own, STEPS, STEPS * EDGE_CAP // 2, EDGE_CAP, 0))(jax.random.split(arg_keys[7], GROUPS * BLOCKS)).reshape((GROUPS, BLOCKS, STEPS)).astype(jnp.int32)
    return dict(src_embed=src_embed, dst_embed=dst_embed, relation=relation, src_index=src_index, dst_index=dst_index, rel_index=rel_index, neg_index=neg_index, edge_count=edge_count)


def tile_terms(src_block, dst_block, relation, src_rows_idx, dst_rows_idx, rel_rows_idx, neg_rows_idx, count):
    slots = src_rows_idx.shape[0]
    negatives = neg_rows_idx.shape[0]
    src_rows = jnp.take(src_block, src_rows_idx, axis=0)
    rel_rows = jnp.take(relation, rel_rows_idx, axis=0)
    query = (src_rows.astype(jnp.float32) * rel_rows).astype(jnp.bfloat16)
    dst_rows = jnp.take(dst_block, dst_rows_idx, axis=0)
    neg_rows = jnp.take(dst_block, neg_rows_idx, axis=0)
    positive = jnp.sum(query.astype(jnp.float32) * dst_rows.astype(jnp.float32), axis=1)
    scores = lax.dot_general(query, neg_rows, (((1,), (1,)), ((), ())), preferred_element_type=jnp.float32)
    live = (jnp.arange(slots, dtype=jnp.int32) < count).astype(jnp.float32)
    dpos = -live * jax.nn.sigmoid(-positive)
    dneg = (jax.nn.sigmoid(scores) * (live[:, None] / negatives)).astype(jnp.bfloat16)
    dquery = dpos[:, None] * dst_rows.astype(jnp.float32) + jnp.dot(dneg, neg_rows, preferred_element_type=jnp.float32)
    neg_grad = lax.dot_general(dneg, query, (((0,), (0,)), ((), ())), preferred_element_type=jnp.float32)
    grad_src = jnp.zeros(src_block.shape, jnp.float32).at[src_rows_idx].add(dquery * rel_rows)
    grad_dst = jnp.zeros(dst_block.shape, jnp.float32).at[dst_rows_idx].add(dpos[:, None] * query.astype(jnp.float32))
    grad_dst = grad_dst.at[neg_rows_idx].add(neg_grad)
    grad_rel = jnp.zeros(relation.shape, jnp.float32).at[rel_rows_idx].add(dquery * src_rows.astype(jnp.float32))
    return grad_src, grad_dst, grad_rel


def reference(src_embed, dst_embed, relation, src_index, dst_index, rel_index, neg_index, edge_count):
    devices_all = GROUPS * BLOCKS
    src_blocks = src_embed.reshape(devices_all, E_DEV, D)
    dst_grid = dst_embed.reshape(GROUPS, BLOCKS, E_DEV, D)
    grad_src = jnp.zeros((devices_all, E_DEV, D), jnp.float32)
    grad_dst = jnp.zeros((GROUPS, BLOCKS, E_DEV, D), jnp.float32)
    rel_total = jnp.zeros((RELS, D), jnp.float32)
    for step in range(STEPS):
        current = jnp.roll(dst_grid, step, axis=1).reshape(devices_all, E_DEV, D)
        items = (src_blocks, current,
                 src_index[:, :, step].reshape(devices_all, EDGE_CAP),
                 dst_index[:, :, step].reshape(devices_all, EDGE_CAP),
                 rel_index[:, :, step].reshape(devices_all, EDGE_CAP),
                 neg_index[:, :, step].reshape(devices_all, NEG),
                 edge_count[:, :, step].reshape(devices_all))

        def visit(carry, item):
            part_src, part_dst, rel_part = tile_terms(item[0], item[1], relation, item[2], item[3], item[4], item[5], item[6])
            return carry + rel_part, (part_src, part_dst)

        rel_total, outputs = lax.scan(visit, rel_total, items)
        grad_src = grad_src + outputs[0]
        grad_dst = grad_dst + jnp.roll(outputs[1].reshape(GROUPS, BLOCKS, E_DEV, D), -step, axis=1)
    return grad_src.reshape(ENTITIES, D), grad_dst.reshape(ENTITIES, D), rel_total
```

```python
import functools

import jax
import jax.numpy as jnp
from jax import lax
from jax.experimental import pallas as pl
from jax.experimental.pallas import tpu as pltpu
from jax.sharding import PartitionSpec as P

MESH = pl.DeviceIdType.MESH
F32 = jnp.float32
BF16 = jnp.bfloat16
NX = 4
NY = 8
ZLO = 2


def nt(a, b):
    return lax.dot_general(a, b, (((1,), (1,)), ((), ())), preferred_element_type=F32)


def nn(a, b):
    return jnp.dot(a, b, preferred_element_type=F32)


def kernel(
    nz, rels, rows_mm, chunk,
    src_hbm, dst_hbm, rel_hbm, si_hbm, di_hbm, ri_hbm, ni_hbm, ec_hbm,
    gs_out, gd_out, rel_out,
    part, src_v, src_far, rel_v, rel_pad, rel_t, src_t, idx, idx_far, ec, ec_far,
    ohs, ohr, sr, rr, qt, gw, gs, gr, gs_send, gs_recv, ga_send, ga_recv, gb_send, gb_recv,
    gh_send, gh_recv, half_recv, xs, x_recv, ys, y_recv, z_all, rel_all,
    in_sem, out_sem, part_send, part_recv, fwd_send, far_send, far_recv,
    g_send, g_recv, h_send, h_recv,
    xs_send, xs_recv, ys_send, ys_recv, zs_send, zs_recv,
    ya_send, ya_recv, xa_send, xa_recv, ca_send, ca_recv,
):
    ent, width = dst_hbm.shape
    half = width // 2
    xrows = NY * chunk
    nchip = ZLO * NY
    grp, blk = lax.axis_index("grp"), lax.axis_index("blk")
    core = lax.rem(blk, 2)
    chip = blk // 2
    y = lax.rem(chip, NY)
    z = (grp // NX) * ZLO + chip // NY
    x = lax.rem(grp, NX)
    even = core == 0
    nxt = lax.rem(chip + 1, nchip) * 2 + core
    prv = lax.rem(chip + nchip - 1, nchip) * 2 + core
    sib = (grp, chip * 2 + 1 - core)

    def at_x(i):
        return ((grp // NX) * NX + i, blk)

    def at_y(i):
        return (grp, (chip // NY) * NY * 2 + i * 2 + core)

    def at_z(i):
        return ((i // ZLO) * NX + x, lax.rem(i, ZLO) * NY * 2 + y * 2 + core)

    x_others = [lax.rem(x + k, NX) for k in range(1, NX)]
    y_others = [lax.rem(y + k, NY) for k in range(1, NY)]
    z_others = [lax.rem(z + k, nz) for k in range(1, nz)]

    def remote(source, target, send, recv, device):
        return pltpu.make_async_remote_copy(
            src_ref=source, dst_ref=target, send_sem=send, recv_sem=recv,
            device_id=device, device_id_type=MESH,
        )

    def arrived(target, recv):
        remote(target, target, recv, recv, sib).wait_recv()

    own = [(si_hbm, 0), (di_hbm, 1), (ri_hbm, 2), (ni_hbm, 3)]
    loads = [
        pltpu.make_async_copy(rel_hbm, rel_v, in_sem.at[0]),
        pltpu.make_async_copy(src_hbm, src_v, in_sem.at[1]),
        pltpu.make_async_copy(dst_hbm, part.at[0], in_sem.at[2]),
        pltpu.make_async_copy(ec_hbm, ec, in_sem.at[3]),
    ] + [pltpu.make_async_copy(ref, idx.at[k], in_sem.at[4 + k]) for ref, k in own]
    for load in loads:
        load.start()

    barrier = pltpu.get_barrier_semaphore()
    greet = [sib, (grp, nxt), (grp, prv)]
    greet += [at_x(i) for i in x_others] + [at_y(i) for i in y_others] + [at_z(i) for i in z_others]
    for device in greet:
        pl.semaphore_signal(barrier, inc=1, device_id=device, device_id_type=MESH)
    pl.semaphore_wait(barrier, len(greet))

    direct = 2 - core
    send_next = remote(
        dst_hbm, part.at[direct], part_send.at[0], part_recv.at[direct], (grp, nxt)
    )
    send_next.start()
    send_sib = remote(dst_hbm, part.at[3], part_send.at[1], part_recv.at[3], sib)
    far = [remote(src_hbm, src_far, far_send.at[0], far_recv.at[0], (grp, prv))]
    far += [remote(ec_hbm, ec_far, far_send.at[1], far_recv.at[1], (grp, prv))]
    far += [
        remote(ref, idx_far.at[k], far_send.at[2 + k], far_recv.at[2 + k], (grp, prv))
        for ref, k in own
    ]

    @pl.when(even)
    def _():
        send_sib.start()
        for copy in far:
            copy.start()

    for load in loads:
        load.wait()

    gr[...] = jnp.zeros_like(gr)
    rel_pad[...] = jnp.zeros_like(rel_pad)
    rel_pad[0:rels, :] = rel_v[...]
    turned = rel_pad[...].T
    high = turned.astype(BF16)
    rel_t[0:width, :] = high
    rel_t[width:, :] = (turned - high.astype(F32)).astype(BF16)
    src_t[...] = src_v[...].T

    def tile_of(w):
        if w in (0, 3):
            return w
        return jnp.where(even, 3 - w, w)

    def row_of(k, w):
        row = idx[k, pl.ds(tile_of(w), 1), :]
        if w == 3:
            row = jnp.where(even, idx_far[k, 3:4, :], row)
        return row

    def live_of(w):
        counts = ec[...].astype(F32)
        if w == 3:
            counts = jnp.where(even, ec_far[...].astype(F32), counts)
        place = lax.broadcasted_iota(jnp.int32, counts.shape, 1)
        count = jnp.sum(jnp.where(place == tile_of(w), counts, 0.0), axis=1, keepdims=True)
        slot = lax.broadcasted_iota(jnp.int32, (1, ent), 1).astype(F32)
        return (slot < count).astype(F32)

    def prepare(w):
        rows = lax.broadcasted_iota(jnp.int32, (ent, ent), 0)
        ohs[w] = (rows == row_of(0, w)).astype(BF16)
        rows = lax.broadcasted_iota(jnp.int32, (rows_mm, ent), 0)
        ohr[w] = (rows == row_of(2, w)).astype(BF16)
        picked = nn(src_t[...], ohs[w])
        both = nn(rel_t[...], ohr[w])
        scale = both[0:width] + both[width:]
        sr[w] = picked
        rr[w] = scale
        qt[w] = (picked * scale).astype(BF16)

    def finish(w, slot):
        block = part[slot]
        scores = nn(block, qt[w])
        rows = lax.broadcasted_iota(jnp.int32, (ent, ent), 0)
        hit = rows == row_of(1, w)
        chosen = (rows == row_of(3, w)).astype(F32)
        weight = jnp.sum(chosen, axis=1, keepdims=True) * (1.0 / ent)
        live = live_of(w)
        pos = jnp.sum(jnp.where(hit, scores, 0.0), axis=0, keepdims=True)
        dpos = -live * jax.nn.sigmoid(-pos)
        terms = jax.nn.sigmoid(scores) * weight * live
        pull = (terms + jnp.where(hit, dpos, 0.0)).astype(BF16)
        dquery = nn(block.T, pull)
        grown = nt(ohr[w], (dquery * sr[w]).astype(BF16))
        gr[0, 0:rows_mm, :] += grown[:, 0:half]
        gr[1, 0:rows_mm, :] += grown[:, half:]
        return pull, dquery

    def spread(w, pull, dquery):
        gw[w] = nt(pull, qt[w])
        return nt(ohs[w], (dquery * rr[w]).astype(BF16))

    prepare(0)
    pull, dquery = finish(0, 0)
    gs[...] = spread(0, pull, dquery)
    prepare(1)
    prepare(2)

    arrived(part.at[direct], part_recv.at[direct])
    forward = remote(
        part.at[direct], part.at[direct], fwd_send.at[0], part_recv.at[direct], sib
    )
    forward.start()

    @pl.when(core == 1)
    def _():
        arrived(part.at[3], part_recv.at[3])

    pull, dquery = finish(1, 2 + core)
    gs[...] += spread(1, pull, dquery)
    gb_send[...] = gw[1].astype(BF16)
    home_copy = remote(gb_send, gb_recv, g_send.at[0], g_recv.at[0], sib)

    @pl.when(core == 1)
    def _():
        home_copy.start()

    @pl.when(even)
    def _():
        for k in range(4):
            arrived(idx_far.at[k], far_recv.at[2 + k])
        arrived(ec_far, far_recv.at[1])
        arrived(src_far, far_recv.at[0])
        src_t[...] = src_far[...].T

    prepare(3)
    other = 1 + core
    arrived(part.at[other], part_recv.at[other])
    pull, dquery = finish(2, 1)
    gs[...] += spread(2, pull, dquery)
    pull, dquery = finish(3, 1 + core)

    swap = remote(
        gr.at[1 - core, pl.ds(0, rows_mm)], half_recv, h_send.at[0], h_recv.at[0], sib
    )
    swap.start()
    last = spread(3, pull, dquery)

    ga_send[...] = (gw[3] + jnp.where(even, gw[2], 0.0)).astype(BF16)
    pair_copy = remote(ga_send, ga_recv, g_send.at[1], g_recv.at[1], sib)
    pair_copy.start()
    gs_send[...] = last.astype(BF16)
    src_copy = remote(gs_send, gs_recv, g_send.at[2], g_recv.at[2], (grp, nxt))

    @pl.when(even)
    def _():
        src_copy.start()

    @pl.when(core == 1)
    def _():
        gs[...] += last

    arrived(half_recv, h_recv.at[0])
    if rows_mm < NX * xrows:
        xs[rows_mm:, :] = jnp.zeros((NX * xrows - rows_mm, half), BF16)
    xs[0:rows_mm, :] = (gr[core, 0:rows_mm, :] + half_recv[...]).astype(BF16)

    sent = [send_next, forward, swap, pair_copy]

    def rows_at(i, size):
        return pl.ds(pl.multiple_of(i * size, size), size)

    for k, i in enumerate(x_others):
        copy = remote(
            xs.at[rows_at(i, xrows)], x_recv.at[x], xs_send.at[k], xs_recv.at[x], at_x(i)
        )
        copy.start()
        sent.append(copy)

    arrived(ga_recv, g_recv.at[1])
    gh_send[...] = (gw[1 + core] + ga_recv[...].astype(F32)).astype(BF16)
    back = remote(gh_send, gh_recv, h_send.at[1], h_recv.at[1], (grp, prv))
    back.start()
    sent.append(back)

    total = xs[rows_at(x, xrows), :].astype(F32)
    for i in x_others:
        arrived(x_recv.at[i], xs_recv.at[i])
        total = total + x_recv[i].astype(F32)
    ys[...] = total.astype(BF16)
    for k, i in enumerate(y_others):
        copy = remote(
            ys.at[rows_at(i, chunk)], y_recv.at[y], ys_send.at[k], ys_recv.at[y], at_y(i)
        )
        copy.start()
        sent.append(copy)

    @pl.when(even)
    def _():
        arrived(gs_recv, g_recv.at[2])
        gs[...] += gs_recv[...].astype(F32)
        arrived(gb_recv, g_recv.at[0])
        gw[0] = gw[0] + gb_recv[...].astype(F32)

    gs_copy = pltpu.make_async_copy(gs, gs_out, out_sem.at[0])
    gs_copy.start()

    total = ys[rows_at(y, chunk), :].astype(F32)
    for i in y_others:
        arrived(y_recv.at[i], ys_recv.at[i])
        total = total + y_recv[i].astype(F32)
    z_all[z] = total
    for k, i in enumerate(z_others):
        copy = remote(z_all.at[z], z_all.at[z], zs_send.at[k], zs_recv.at[z], at_z(i))
        copy.start()
        sent.append(copy)

    arrived(gh_recv, h_recv.at[1])
    gw[0] = gw[0] + gh_recv[...].astype(F32)
    gd_copy = pltpu.make_async_copy(gw.at[0], gd_out, out_sem.at[1])
    gd_copy.start()

    for i in z_others:
        arrived(z_all.at[i], zs_recv.at[i])
    total = z_all[0]
    for i in range(1, nz):
        total = total + z_all[i]
    rel_all[core, x, y] = total.astype(BF16)
    for k, i in enumerate(y_others):
        piece = rel_all.at[core, x, y]
        copy = remote(piece, piece, ya_send.at[k], ya_recv.at[y], at_y(i))
        copy.start()
        sent.append(copy)
    for i in y_others:
        arrived(rel_all.at[core, x, i], ya_recv.at[i])
    for k, i in enumerate(x_others):
        piece = rel_all.at[core, x]
        copy = remote(piece, piece, xa_send.at[k], xa_recv.at[x], at_x(i))
        copy.start()
        sent.append(copy)
    for k, i in enumerate([x] + x_others):
        piece = rel_all.at[core, i]
        if k > 0:
            arrived(piece, xa_recv.at[i])
        copy = remote(piece, piece, ca_send.at[k], ca_recv.at[i], sib)
        copy.start()
        sent.append(copy)
    for i in range(NX):
        arrived(rel_all.at[1 - core, i], ca_recv.at[i])
    rel_copy = pltpu.make_async_copy(rel_all, rel_out, out_sem.at[2])
    rel_copy.start()

    for copy in sent:
        copy.wait_send()

    @pl.when(even)
    def _():
        send_sib.wait_send()
        for copy in far:
            copy.wait_send()
        src_copy.wait_send()

    @pl.when(core == 1)
    def _():
        home_copy.wait_send()

    gs_copy.wait()
    gd_copy.wait()
    rel_copy.wait()


def body(src_embed, dst_embed, relation, src_index, dst_index, rel_index, neg_index, edge_count):
    ent, width = src_embed.shape
    rels = relation.shape[0]
    steps = src_index.shape[2]
    nz = lax.axis_size("grp") // NX * ZLO
    half = width // 2
    chunk = -(-rels // (NX * NY * 16)) * 16
    rows_mm = -(-rels // 128) * 128
    xrows = NY * chunk
    tables = [t.reshape(steps, ent) for t in (src_index, dst_index, rel_index, neg_index)]
    vmem = pltpu.VMEM
    dma = pltpu.SemaphoreType.DMA
    scratch = [
        vmem((4, ent, width), BF16),
        vmem((ent, width), BF16),
        vmem((ent, width), BF16),
        vmem((rels, width), F32),
        vmem((rows_mm, width), F32),
        vmem((2 * width, rows_mm), BF16),
        vmem((width, ent), BF16),
        vmem((4, steps, ent), jnp.int32),
        vmem((4, steps, ent), jnp.int32),
        vmem((1, steps), jnp.int32),
        vmem((1, steps), jnp.int32),
        vmem((4, ent, ent), BF16),
        vmem((4, rows_mm, ent), BF16),
        vmem((4, width, ent), F32),
        vmem((4, width, ent), F32),
        vmem((4, width, ent), BF16),
        vmem((4, ent, width), F32),
        vmem((ent, width), F32),
        vmem((2, rows_mm, half), F32),
        vmem((ent, width), BF16),
        vmem((ent, width), BF16),
        vmem((ent, width), BF16),
        vmem((ent, width), BF16),
        vmem((ent, width), BF16),
        vmem((ent, width), BF16),
        vmem((ent, width), BF16),
        vmem((ent, width), BF16),
        vmem((rows_mm, half), F32),
        vmem((NX * xrows, half), BF16),
        vmem((NX, xrows, half), BF16),
        vmem((xrows, half), BF16),
        vmem((NY, chunk, half), BF16),
        vmem((nz, chunk, half), F32),
        vmem((2, NX, NY, chunk, half), BF16),
        dma((8,)),
        dma((3,)),
        dma((2,)),
        dma((4,)),
        dma((1,)),
        dma((6,)),
        dma((6,)),
        dma((3,)),
        dma((3,)),
        dma((2,)),
        dma((2,)),
        dma((NX,)), dma((NX,)),
        dma((NY,)), dma((NY,)),
        dma((nz,)), dma((nz,)),
        dma((NY,)), dma((NY,)),
        dma((NX,)), dma((NX,)),
        dma((NX,)), dma((NX,)),
    ]
    grad_src, grad_dst, rel_parts = pl.pallas_call(
        functools.partial(kernel, nz, rels, rows_mm, chunk),
        out_shape=(
            jax.ShapeDtypeStruct((ent, width), F32),
            jax.ShapeDtypeStruct((ent, width), F32),
            jax.ShapeDtypeStruct((2, NX, NY, chunk, half), BF16),
        ),
        in_specs=[pl.BlockSpec(memory_space=pl.ANY)] * 8,
        out_specs=(pl.BlockSpec(memory_space=pl.ANY),) * 3,
        scratch_shapes=scratch,
        compiler_params=pltpu.CompilerParams(
            collective_id=0, has_side_effects=True, vmem_limit_bytes=56 * 1024 * 1024
        ),
    )(src_embed, dst_embed, relation, *tables, edge_count.reshape(1, steps))
    rel_parts = rel_parts.reshape(2, NX * xrows, half)[:, :rels]
    grad_rel = jnp.concatenate([rel_parts[0], rel_parts[1]], axis=1).astype(F32)
    return (grad_src, grad_dst, grad_rel)


def solution(mesh):
    in_specs = (
        P(("grp", "blk"), None),
        P(("grp", "blk"), None),
        P(),
        P("grp", "blk", None, None),
        P("grp", "blk", None, None),
        P("grp", "blk", None, None),
        P("grp", "blk", None, None),
        P("grp", "blk", None),
    )
    out_specs = (P(("grp", "blk"), None), P(("grp", "blk"), None), P())
    return jax.shard_map(body, mesh=mesh, in_specs=in_specs, out_specs=out_specs, check_vma=False)
```

```python
import functools

import jax
import jax.numpy as jnp
from jax import lax
from jax.experimental import pallas as pl
from jax.experimental.pallas import tpu as pltpu
from jax.sharding import PartitionSpec as P

MESH = pl.DeviceIdType.MESH
F32 = jnp.float32
BF16 = jnp.bfloat16
NX = 4
NY = 8
ZLO = 2
CHUNK = 16


def nt(a, b):
    return lax.dot_general(a, b, (((1,), (1,)), ((), ())), preferred_element_type=F32)


def nn(a, b):
    return jnp.dot(a, b, preferred_element_type=F32)


def kernel(
    nz, rels, rows_mm, pieces,
    src_hbm, dst_hbm, rel_hbm, si_hbm, di_hbm, ri_hbm, ni_hbm, ec_hbm,
    gs_out, gd_out, rel_out,
    part, src_v, src_far, rel_v, rel_pad, rel_t, src_t, idx, idx_far, ec, ec_far,
    ohs, ohr, sr, rr, qt, weight, pulls, back_v, gw, gs, gr,
    gs_send, gs_recv, ga_send, ga_recv, gb_send, gb_recv, gh_send, gh_recv,
    half_recv, xs, x_recv, ys, y_recv, z_all, rel_all,
    in_sem, out_sem, part_send, part_recv, fwd_send, far_send, far_recv,
    g_send, g_recv, h_send, h_recv, s_send, s_recv,
    xs_send, xs_recv, ys_send, ys_recv, zs_send, zs_recv,
    ya_send, ya_recv, xa_send, xa_recv, ca_send, ca_recv,
):
    ent, width = dst_hbm.shape
    half = width // 2
    yrows = CHUNK
    xrows = NY * yrows
    prows = NX * xrows
    nchip = ZLO * NY
    grp, blk = lax.axis_index("grp"), lax.axis_index("blk")
    core = lax.rem(blk, 2)
    chip = blk // 2
    y = lax.rem(chip, NY)
    z = (grp // NX) * ZLO + chip // NY
    x = lax.rem(grp, NX)
    even = core == 0
    nxt = lax.rem(chip + 1, nchip) * 2 + core
    prv = lax.rem(chip + nchip - 1, nchip) * 2 + core
    sib = (grp, chip * 2 + 1 - core)

    def at_x(i):
        return ((grp // NX) * NX + i, blk)

    def at_y(i):
        return (grp, (chip // NY) * NY * 2 + i * 2 + core)

    def at_z(i):
        return ((i // ZLO) * NX + x, lax.rem(i, ZLO) * NY * 2 + y * 2 + core)

    x_others = [lax.rem(x + k, NX) for k in range(1, NX)]
    y_others = [lax.rem(y + k, NY) for k in range(1, NY)]
    z_others = [lax.rem(z + k, nz) for k in range(1, nz)]

    def remote(source, target, send, recv, device):
        return pltpu.make_async_remote_copy(
            src_ref=source, dst_ref=target, send_sem=send, recv_sem=recv,
            device_id=device, device_id_type=MESH,
        )

    def arrived(target, recv):
        remote(target, target, recv, recv, sib).wait_recv()

    barrier = pltpu.get_barrier_semaphore()
    greet = [sib, (grp, nxt), (grp, prv)]
    greet += [at_x(i) for i in x_others] + [at_y(i) for i in y_others] + [at_z(i) for i in z_others]
    for device in greet:
        pl.semaphore_signal(barrier, inc=1, device_id=device, device_id_type=MESH)

    own = [(si_hbm, 0), (di_hbm, 1), (ri_hbm, 2), (ni_hbm, 3)]
    loads = [
        pltpu.make_async_copy(rel_hbm, rel_v, in_sem.at[0]),
        pltpu.make_async_copy(src_hbm, src_v, in_sem.at[1]),
        pltpu.make_async_copy(dst_hbm, part.at[0], in_sem.at[2]),
        pltpu.make_async_copy(ec_hbm, ec, in_sem.at[3]),
    ] + [pltpu.make_async_copy(ref, idx.at[k], in_sem.at[4 + k]) for ref, k in own]
    for load in loads:
        load.start()
    if rows_mm < pieces * prows:
        gr[:, rows_mm:, :] = jnp.zeros((2, pieces * prows - rows_mm, half), F32)
    tail = rels // 8 * 8
    rel_pad[tail:, :] = jnp.zeros((rows_mm - tail, width), F32)
    for load in loads:
        load.wait()
    rel_pad[0:rels, :] = rel_v[...]
    rel_t[...] = rel_pad[...].astype(BF16).T
    src_t[...] = src_v[...].T

    pl.semaphore_wait(barrier, len(greet))

    direct = 2 - core
    send_next = remote(
        dst_hbm, part.at[direct], part_send.at[0], part_recv.at[direct], (grp, nxt)
    )
    send_next.start()
    send_sib = remote(dst_hbm, part.at[3], part_send.at[1], part_recv.at[3], sib)
    far = [remote(src_hbm, src_far, far_send.at[0], far_recv.at[0], (grp, prv))]
    far += [remote(ec_hbm, ec_far, far_send.at[1], far_recv.at[1], (grp, prv))]
    far += [
        remote(ref, idx_far.at[k], far_send.at[2 + k], far_recv.at[2 + k], (grp, prv))
        for ref, k in own
    ]

    @pl.when(even)
    def _():
        send_sib.start()
        for copy in far:
            copy.start()

    def tile_of(w):
        if w in (0, 3):
            return w
        return jnp.where(even, 3 - w, w)

    def row_of(k, w):
        row = idx[k, pl.ds(tile_of(w), 1), :]
        if w == 3:
            row = jnp.where(even, idx_far[k, 3:4, :], row)
        return row

    def live_of(w):
        counts = ec[...].astype(F32)
        if w == 3:
            counts = jnp.where(even, ec_far[...].astype(F32), counts)
        place = lax.broadcasted_iota(jnp.int32, counts.shape, 1)
        count = jnp.sum(jnp.where(place == tile_of(w), counts, 0.0), axis=1, keepdims=True)
        slot = lax.broadcasted_iota(jnp.int32, (1, ent), 1).astype(F32)
        return slot < count

    def prepare(w):
        rows = lax.broadcasted_iota(jnp.int32, (ent, ent), 0)
        ohs[w] = (rows == jnp.where(live_of(w), row_of(0, w), -1)).astype(BF16)
        chosen = (rows == row_of(3, w)).astype(F32)
        weight[w] = jnp.sum(chosen, axis=1, keepdims=True) * (1.0 / ent)
        rows = lax.broadcasted_iota(jnp.int32, (rows_mm, ent), 0)
        ohr[w] = (rows == row_of(2, w)).astype(BF16)
        picked = nn(src_t[...], ohs[w])
        scale = nn(rel_t[...], ohr[w])
        sr[w] = picked.astype(BF16)
        rr[w] = scale.astype(BF16)
        qt[w] = (picked * scale).astype(BF16)

    def finish(w, slot):
        block = part[slot]
        scores = nn(block, qt[w])
        rows = lax.broadcasted_iota(jnp.int32, (ent, ent), 0)
        hit = rows == row_of(1, w)
        pos = jnp.sum(jnp.where(hit, scores, 0.0), axis=0, keepdims=True)
        dpos = -jax.nn.sigmoid(-pos)
        terms = pl.reciprocal(1.0 + jnp.exp(-scores), approx=True) * weight[w]
        pull = (terms + jnp.where(hit, dpos, 0.0)).astype(BF16)
        pulls[w] = pull
        dquery = nn(block.T, pull)
        back_v[w] = (dquery * rr[w].astype(F32)).astype(BF16)
        value = (dquery * sr[w].astype(F32)).astype(BF16)
        for p in range(pieces):
            low, high = p * prows, min((p + 1) * prows, rows_mm)
            grown = nt(ohr[w, low:high, :], value)
            for h in range(2):
                grown_half = grown[:, h * half:(h + 1) * half]
                if w == 0:
                    gr[h, low:high, :] = grown_half
                else:
                    gr[h, low:high, :] += grown_half
            if w == 3:
                swaps[p].start()

    def spread(w):
        gw[w] = nt(pulls[w], qt[w])
        return nt(ohs[w], back_v[w])

    swaps = [
        remote(
            gr.at[1 - core, pl.ds(p * prows, prows)], half_recv.at[p],
            s_send.at[p], s_recv.at[p], sib,
        )
        for p in range(pieces)
    ]

    prepare(0)
    finish(0, 0)
    prepare(1)
    prepare(2)

    arrived(part.at[direct], part_recv.at[direct])
    forward = remote(
        part.at[direct], part.at[direct], fwd_send.at[0], part_recv.at[direct], sib
    )
    forward.start()

    @pl.when(even)
    def _():
        for k in range(4):
            arrived(idx_far.at[k], far_recv.at[2 + k])
        arrived(ec_far, far_recv.at[1])
        arrived(src_far, far_recv.at[0])
        src_t[...] = src_far[...].T

    @pl.when(core == 1)
    def _():
        arrived(part.at[3], part_recv.at[3])

    prepare(3)
    finish(1, 2 + core)
    other = 1 + core
    arrived(part.at[other], part_recv.at[other])
    finish(2, 1)
    finish(3, 1 + core)

    sent = [send_next, forward] + swaps

    def rows_at(i, size):
        return pl.ds(pl.multiple_of(i * size, size), size)

    gs[...] = spread(0) + spread(1)
    for p in range(pieces):
        arrived(half_recv.at[p], s_recv.at[p])
        xs[p] = (gr[core, p * prows:(p + 1) * prows, :] + half_recv[p]).astype(BF16)
        for k, i in enumerate(x_others):
            copy = remote(
                xs.at[p, rows_at(i, xrows)], x_recv.at[p, x],
                xs_send.at[p, k], xs_recv.at[p, x], at_x(i),
            )
            copy.start()
            sent.append(copy)

    gs[...] += spread(2)
    last = spread(3)
    gb_send[...] = gw[1].astype(BF16)
    home_copy = remote(gb_send, gb_recv, g_send.at[0], g_recv.at[0], sib)
    ga_send[...] = (gw[3] + jnp.where(even, gw[2], 0.0)).astype(BF16)
    pair_copy = remote(ga_send, ga_recv, g_send.at[1], g_recv.at[1], sib)
    pair_copy.start()
    sent.append(pair_copy)
    gs_send[...] = last.astype(BF16)
    src_copy = remote(gs_send, gs_recv, g_send.at[2], g_recv.at[2], (grp, nxt))

    @pl.when(even)
    def _():
        src_copy.start()

    @pl.when(core == 1)
    def _():
        home_copy.start()
        gs[...] += last

    for p in range(pieces):
        total = xs[p, rows_at(x, xrows), :].astype(F32)
        for i in x_others:
            arrived(x_recv.at[p, i], xs_recv.at[p, i])
            total = total + x_recv[p, i].astype(F32)
        ys[p] = total.astype(BF16)
        for k, i in enumerate(y_others):
            copy = remote(
                ys.at[p, rows_at(i, yrows)], y_recv.at[p, y],
                ys_send.at[p, k], ys_recv.at[p, y], at_y(i),
            )
            copy.start()
            sent.append(copy)

    arrived(ga_recv, g_recv.at[1])
    gh_send[...] = (gw[1 + core] + ga_recv[...].astype(F32)).astype(BF16)
    homeward = remote(gh_send, gh_recv, h_send.at[0], h_recv.at[0], (grp, prv))
    homeward.start()
    sent.append(homeward)

    for p in range(pieces):
        total = ys[p, rows_at(y, yrows), :].astype(F32)
        for i in y_others:
            arrived(y_recv.at[p, i], ys_recv.at[p, i])
            total = total + y_recv[p, i].astype(F32)
        z_all[p, z] = total
        for k, i in enumerate(z_others):
            copy = remote(
                z_all.at[p, z], z_all.at[p, z], zs_send.at[p, k], zs_recv.at[p, z], at_z(i)
            )
            copy.start()
            sent.append(copy)

    @pl.when(even)
    def _():
        arrived(gs_recv, g_recv.at[2])
        gs[...] += gs_recv[...].astype(F32)
        arrived(gb_recv, g_recv.at[0])
        gw[0] = gw[0] + gb_recv[...].astype(F32)

    gs_copy = pltpu.make_async_copy(gs, gs_out, out_sem.at[0])
    gs_copy.start()

    for p in range(pieces):
        for i in z_others:
            arrived(z_all.at[p, i], zs_recv.at[p, i])
        total = z_all[p, 0]
        for i in range(1, nz):
            total = total + z_all[p, i]
        piece = rel_all.at[core, p, x, y]
        piece[...] = total.astype(BF16)
        for k, i in enumerate(y_others):
            copy = remote(piece, piece, ya_send.at[p, k], ya_recv.at[p, y], at_y(i))
            copy.start()
            sent.append(copy)

    arrived(gh_recv, h_recv.at[0])
    gw[0] = gw[0] + gh_recv[...].astype(F32)
    gd_copy = pltpu.make_async_copy(gw.at[0], gd_out, out_sem.at[1])
    gd_copy.start()

    for p in range(pieces):
        for i in y_others:
            arrived(rel_all.at[core, p, x, i], ya_recv.at[p, i])
        piece = rel_all.at[core, p, x]
        for k, i in enumerate(x_others):
            copy = remote(piece, piece, xa_send.at[p, k], xa_recv.at[p, x], at_x(i))
            copy.start()
            sent.append(copy)
    for p in range(pieces):
        for i in x_others:
            arrived(rel_all.at[core, p, i], xa_recv.at[p, i])
        piece = rel_all.at[core, p]
        copy = remote(piece, piece, ca_send.at[p], ca_recv.at[p], sib)
        copy.start()
        sent.append(copy)
    rel_copies = []
    for p in range(pieces):
        arrived(rel_all.at[1 - core, p], ca_recv.at[p])
        for h in range(2):
            copy = pltpu.make_async_copy(
                rel_all.at[h, p], rel_out.at[h, p], out_sem.at[2 + 2 * p + h]
            )
            copy.start()
            rel_copies.append(copy)

    for copy in sent:
        copy.wait_send()

    @pl.when(even)
    def _():
        send_sib.wait_send()
        for copy in far:
            copy.wait_send()
        src_copy.wait_send()

    @pl.when(core == 1)
    def _():
        home_copy.wait_send()

    gs_copy.wait()
    gd_copy.wait()
    for copy in rel_copies:
        copy.wait()


def store_kernel(
    rels, gs_in, gd_in, rel_in, gs_out, gd_out, rel_out, rel_b, rel_f, gs_v, gd_v, in_sem, out_sem
):
    ins = [
        pltpu.make_async_copy(rel_in, rel_b, in_sem.at[0]),
        pltpu.make_async_copy(gs_in, gs_v, in_sem.at[1]),
        pltpu.make_async_copy(gd_in, gd_v, in_sem.at[2]),
    ]
    outs = [
        pltpu.make_async_copy(rel_f, rel_out, out_sem.at[0]),
        pltpu.make_async_copy(gs_v, gs_out, out_sem.at[1]),
        pltpu.make_async_copy(gd_v, gd_out, out_sem.at[2]),
    ]
    for copy in ins:
        copy.start()
    half = rel_b.shape[2]
    ins[0].wait()
    for h in range(2):
        rel_f[:, h * half:(h + 1) * half] = rel_b[h, 0:rels, :].astype(F32)
    outs[0].start()
    for k in (1, 2):
        ins[k].wait()
        outs[k].start()
    for copy in outs:
        copy.wait()


def body(src_embed, dst_embed, relation, src_index, dst_index, rel_index, neg_index, edge_count):
    ent, width = src_embed.shape
    rels = relation.shape[0]
    steps = src_index.shape[2]
    nz = lax.axis_size("grp") // NX * ZLO
    half = width // 2
    pieces = -(-rels // (NX * NY * CHUNK))
    rows_mm = -(-rels // 128) * 128
    xrows = NY * CHUNK
    prows = NX * xrows
    tables = [t.reshape(steps, ent) for t in (src_index, dst_index, rel_index, neg_index)]
    vmem = pltpu.VMEM
    dma = pltpu.SemaphoreType.DMA
    block = vmem((ent, width), BF16)
    scratch = [
        vmem((4, ent, width), BF16),
        block,
        block,
        vmem((rels, width), F32),
        vmem((rows_mm, width), F32),
        vmem((width, rows_mm), BF16),
        vmem((width, ent), BF16),
        vmem((4, steps, ent), jnp.int32),
        vmem((4, steps, ent), jnp.int32),
        vmem((1, steps), jnp.int32),
        vmem((1, steps), jnp.int32),
        vmem((4, ent, ent), BF16),
        vmem((4, rows_mm, ent), BF16),
        vmem((4, width, ent), BF16),
        vmem((4, width, ent), BF16),
        vmem((4, width, ent), BF16),
        vmem((4, ent, 1), F32),
        vmem((4, ent, ent), BF16),
        vmem((4, width, ent), BF16),
        vmem((4, ent, width), F32),
        vmem((ent, width), F32),
        vmem((2, pieces * prows, half), F32),
        block, block, block, block, block, block, block, block,
        vmem((pieces, prows, half), F32),
        vmem((pieces, prows, half), BF16),
        vmem((pieces, NX, xrows, half), BF16),
        vmem((pieces, xrows, half), BF16),
        vmem((pieces, NY, CHUNK, half), BF16),
        vmem((pieces, nz, CHUNK, half), F32),
        vmem((2, pieces, NX, NY, CHUNK, half), BF16),
        dma((8,)),
        dma((2 + 2 * pieces,)),
        dma((2,)),
        dma((4,)),
        dma((1,)),
        dma((6,)),
        dma((6,)),
        dma((3,)),
        dma((3,)),
        dma((1,)),
        dma((1,)),
        dma((pieces,)), dma((pieces,)),
        dma((pieces, NX)), dma((pieces, NX)),
        dma((pieces, NY)), dma((pieces, NY)),
        dma((pieces, nz)), dma((pieces, nz)),
        dma((pieces, NY)), dma((pieces, NY)),
        dma((pieces, NX)), dma((pieces, NX)),
        dma((pieces,)), dma((pieces,)),
    ]
    anywhere = pl.BlockSpec(memory_space=pl.ANY)
    grad = jax.ShapeDtypeStruct((ent, width), F32)
    grad_src, grad_dst, rel_parts = pl.pallas_call(
        functools.partial(kernel, nz, rels, rows_mm, pieces),
        out_shape=(
            grad, grad, jax.ShapeDtypeStruct((2, pieces, NX, NY, CHUNK, half), BF16)
        ),
        in_specs=[anywhere] * 8,
        out_specs=(anywhere,) * 3,
        scratch_shapes=scratch,
        compiler_params=pltpu.CompilerParams(
            collective_id=0, has_side_effects=True, vmem_limit_bytes=56 * 1024 * 1024
        ),
    )(src_embed, dst_embed, relation, *tables, edge_count.reshape(1, steps))
    rel_parts = rel_parts.reshape(2, pieces * prows, half)
    return pl.pallas_call(
        functools.partial(store_kernel, rels),
        out_shape=(grad, grad, jax.ShapeDtypeStruct((rels, width), F32)),
        in_specs=[anywhere] * 3,
        out_specs=(anywhere,) * 3,
        scratch_shapes=[
            vmem(rel_parts.shape, BF16), vmem((rels, width), F32),
            vmem((ent, width), F32), vmem((ent, width), F32), dma((3,)), dma((3,)),
        ],
        compiler_params=pltpu.CompilerParams(vmem_limit_bytes=16 * 1024 * 1024),
    )(grad_src, grad_dst, rel_parts)


def solution(mesh):
    in_specs = (
        P(("grp", "blk"), None),
        P(("grp", "blk"), None),
        P(),
        P("grp", "blk", None, None),
        P("grp", "blk", None, None),
        P("grp", "blk", None, None),
        P("grp", "blk", None, None),
        P("grp", "blk", None),
    )
    out_specs = (P(("grp", "blk"), None), P(("grp", "blk"), None), P())
    return jax.shard_map(body, mesh=mesh, in_specs=in_specs, out_specs=out_specs, check_vma=False)
```

```python
import functools

import jax
import jax.numpy as jnp
from jax import lax
from jax.experimental import pallas as pl
from jax.experimental.pallas import tpu as pltpu
from jax.sharding import PartitionSpec as P

MESH = pl.DeviceIdType.MESH
F32 = jnp.float32
BF16 = jnp.bfloat16
NX = 4
NY = 8
ZLO = 2
CHUNK = 16
STEP = 128


def nt(a, b):
    return lax.dot_general(a, b, (((1,), (1,)), ((), ())), preferred_element_type=F32)


def nn(a, b):
    return jnp.dot(a, b, preferred_element_type=F32)


def kernel(
    nz, rels, rows_mm, pieces,
    src_hbm, dst_hbm, rel_hbm, si_hbm, di_hbm, ri_hbm, ni_hbm, ec_hbm,
    gs_out, gd_out, rel_out,
    part, src_v, src_far, rel_v, rel_pad, rel_t, src_t, idx, idx_far, ec, ec_far,
    ohs, ohr, sr, rr, qt, weight, pulls, back_v, gw, gs, gr,
    gs_send, gs_recv, ga_send, ga_recv, gb_send, gb_recv, gh_send, gh_recv,
    half_recv, xs, x_recv, ys, y_recv, z_all, rel_own,
    in_sem, out_sem, part_send, part_recv, far_send, far_recv,
    g_send, g_recv, s_send, s_recv,
    xs_send, xs_recv, ys_send, ys_recv, zs_send, zs_recv,
    ya_send, ya_recv, xa_send, xa_recv, ca_send, ca_recv,
):
    ent, width = dst_hbm.shape
    half = width // 2
    yrows = CHUNK
    xrows = NY * yrows
    prows = NX * xrows
    nchip = ZLO * NY
    grp, blk = lax.axis_index("grp"), lax.axis_index("blk")
    core = lax.rem(blk, 2)
    chip = blk // 2
    y = lax.rem(chip, NY)
    z = (grp // NX) * ZLO + chip // NY
    x = lax.rem(grp, NX)
    even = core == 0
    nxt = lax.rem(chip + 1, nchip) * 2 + core
    prv = lax.rem(chip + nchip - 1, nchip) * 2 + core
    sib = (grp, chip * 2 + 1 - core)

    def at_x(i):
        return ((grp // NX) * NX + i, blk)

    def at_y(i):
        return (grp, (chip // NY) * NY * 2 + i * 2 + core)

    def at_z(i):
        return ((i // ZLO) * NX + x, lax.rem(i, ZLO) * NY * 2 + y * 2 + core)

    x_others = [lax.rem(x + k, NX) for k in range(1, NX)]
    y_others = [lax.rem(y + k, NY) for k in range(1, NY)]
    z_others = [lax.rem(z + k, nz) for k in range(1, nz)]

    def remote(source, target, send, recv, device):
        return pltpu.make_async_remote_copy(
            src_ref=source, dst_ref=target, send_sem=send, recv_sem=recv,
            device_id=device, device_id_type=MESH,
        )

    def arrived(buffer, recv):
        pltpu.make_async_copy(buffer, buffer, recv).wait()

    barrier = pltpu.get_barrier_semaphore()
    greet = [sib, (grp, nxt), (grp, prv)]
    greet += [at_x(i) for i in x_others] + [at_y(i) for i in y_others] + [at_z(i) for i in z_others]
    for device in greet:
        pl.semaphore_signal(barrier, inc=1, device_id=device, device_id_type=MESH)

    own = [(si_hbm, 0), (di_hbm, 1), (ri_hbm, 2), (ni_hbm, 3)]
    loads = [
        pltpu.make_async_copy(rel_hbm, rel_v, in_sem.at[0]),
        pltpu.make_async_copy(src_hbm, src_v, in_sem.at[1]),
        pltpu.make_async_copy(dst_hbm, part.at[0], in_sem.at[2]),
        pltpu.make_async_copy(ec_hbm, ec, in_sem.at[3]),
    ]
    for load in loads + [pltpu.make_async_copy(ref, idx.at[k], in_sem.at[4]) for ref, k in own]:
        load.start()
    if rows_mm < pieces * prows:
        gr[:, rows_mm:, :] = jnp.zeros((2, pieces * prows - rows_mm, half), F32)
    tail = rels // 8 * 8
    rel_pad[tail:, :] = jnp.zeros((rows_mm - tail, width), F32)
    for load in loads:
        load.wait()
    arrived(idx, in_sem.at[4])
    rel_pad[0:rels, :] = rel_v[...]
    turned = rel_pad[...].T
    high = turned.astype(BF16)
    rel_t[0:width, :] = high
    rel_t[width:, :] = (turned - high.astype(F32)).astype(BF16)
    src_t[...] = src_v[...].T

    pl.semaphore_wait(barrier, len(greet))

    direct = 2 - core
    send_next = remote(
        dst_hbm, part.at[direct], part_send.at[0], part_recv.at[direct], (grp, nxt)
    )
    send_next.start()
    send_sib = remote(dst_hbm, part.at[3], part_send.at[1], part_recv.at[3], sib)
    far = [remote(src_hbm, src_far, far_send.at[0], far_recv.at[0], (grp, prv))]
    far += [remote(ec_hbm, ec_far, far_send.at[1], far_recv.at[1], (grp, prv))]
    far += [
        remote(ref, idx_far.at[k], far_send.at[2], far_recv.at[2], (grp, prv))
        for ref, k in own
    ]

    @pl.when(even)
    def _():
        send_sib.start()
        for copy in far:
            copy.start()

    def tile_of(w):
        if w in (0, 3):
            return w
        return jnp.where(even, 3 - w, w)

    def row_of(k, w):
        row = idx[k, pl.ds(tile_of(w), 1), :]
        if w == 3:
            row = jnp.where(even, idx_far[k, 3:4, :], row)
        return row

    def live_of(w):
        counts = ec[...].astype(F32)
        if w == 3:
            counts = jnp.where(even, ec_far[...].astype(F32), counts)
        place = lax.broadcasted_iota(jnp.int32, counts.shape, 1)
        count = jnp.sum(jnp.where(place == tile_of(w), counts, 0.0), axis=1, keepdims=True)
        slot = lax.broadcasted_iota(jnp.int32, (1, ent), 1).astype(F32)
        return slot < count

    def prepare(w):
        rows = lax.broadcasted_iota(jnp.int32, (ent, ent), 0)
        ohs[w] = (rows == jnp.where(live_of(w), row_of(0, w), -1)).astype(BF16)
        chosen = (rows == row_of(3, w)).astype(F32)
        weight[w] = jnp.sum(chosen, axis=1, keepdims=True) * (1.0 / ent)
        rows = lax.broadcasted_iota(jnp.int32, (rows_mm, ent), 0)
        ohr[w] = (rows == row_of(2, w)).astype(BF16)
        picked = nn(src_t[...], ohs[w])
        both = nn(rel_t[...], ohr[w])
        scale = both[0:width] + both[width:]
        sr[w] = picked.astype(BF16)
        rr[w] = scale
        qt[w] = (picked * scale).astype(BF16)

    def finish(w, slot):
        block = part[slot]
        for low in range(0, ent, STEP):
            scores = nn(block[low:low + STEP], qt[w])
            rows = low + lax.broadcasted_iota(jnp.int32, (STEP, ent), 0)
            decay = jnp.exp(jnp.minimum(-scores, 87.0))
            share = weight[w, low:low + STEP]
            share = jnp.where(rows == row_of(1, w), share - decay, share)
            pulls[w, low:low + STEP] = (pl.reciprocal(1.0 + decay, approx=True) * share).astype(BF16)
        pull = pulls[w]
        dquery = nn(block.T, pull)
        back_v[w] = (dquery * rr[w]).astype(BF16)
        value = (dquery * sr[w].astype(F32)).astype(BF16)
        for p in range(pieces):
            low, high = p * prows, min((p + 1) * prows, rows_mm)
            grown = nt(ohr[w, low:high, :], value)
            for h in range(2):
                grown_half = grown[:, h * half:(h + 1) * half]
                if w == 0:
                    gr[h, low:high, :] = grown_half
                else:
                    gr[h, low:high, :] += grown_half
            if w == 3:
                swaps[p].start()

    def spread(w):
        gw[w] = nt(pulls[w], qt[w])
        return nt(ohs[w], back_v[w])

    swaps = [
        remote(
            gr.at[1 - core, pl.ds(p * prows, prows)], half_recv.at[p],
            s_send.at[p], s_recv.at[p], sib,
        )
        for p in range(pieces)
    ]

    prepare(0)
    finish(0, 0)
    prepare(1)
    prepare(2)

    arrived(part.at[direct], part_recv.at[direct])
    forward = remote(
        part.at[direct], part.at[direct], part_send.at[2], part_recv.at[direct], sib
    )
    forward.start()

    @pl.when(even)
    def _():
        arrived(idx_far, far_recv.at[2])
        arrived(ec_far, far_recv.at[1])
        arrived(src_far, far_recv.at[0])
        src_t[...] = src_far[...].T

    @pl.when(core == 1)
    def _():
        arrived(part.at[3], part_recv.at[3])

    prepare(3)
    finish(1, 2 + core)
    other = 1 + core
    arrived(part.at[other], part_recv.at[other])
    finish(2, 1)
    finish(3, 1 + core)

    sent = [send_next, forward] + swaps

    def rows_at(i, size):
        return pl.ds(pl.multiple_of(i * size, size), size)

    gs[...] = spread(0) + spread(1)
    for p in range(pieces):
        arrived(half_recv.at[p], s_recv.at[p])
        xs[p] = (gr[core, p * prows:(p + 1) * prows, :] + half_recv[p]).astype(BF16)
        for k, i in enumerate(x_others):
            remote(
                xs.at[p, rows_at(i, xrows)], x_recv.at[p, k], xs_send.at[p], xs_recv.at[p], at_x(i)
            ).start()

    gs[...] += spread(2)
    last = spread(3)
    ga_send[...] = (gw[3] + jnp.where(even, gw[2], 0.0)).astype(BF16)
    pair_copy = remote(ga_send, ga_recv, g_send.at[1], g_recv.at[1], sib)
    pair_copy.start()
    gs_send[...] = last.astype(BF16)
    src_copy = remote(gs_send, gs_recv, g_send.at[2], g_recv.at[2], (grp, nxt))
    gb_send[...] = gw[1].astype(BF16)
    home_copy = remote(gb_send, gb_recv, g_send.at[0], g_recv.at[0], sib)

    @pl.when(even)
    def _():
        src_copy.start()

    @pl.when(core == 1)
    def _():
        home_copy.start()
        gs[...] += last

    arrived(ga_recv, g_recv.at[1])
    gh_send[...] = (gw[1 + core] + ga_recv[...].astype(F32)).astype(BF16)
    homeward = remote(gh_send, gh_recv, g_send.at[3], g_recv.at[3], (grp, prv))
    homeward.start()
    sent += [pair_copy, homeward]

    for p in range(pieces):
        total = xs[p, rows_at(x, xrows), :].astype(F32)
        arrived(x_recv.at[p], xs_recv.at[p])
        for k in range(NX - 1):
            total = total + x_recv[p, k].astype(F32)
        ys[p] = total.astype(BF16)
        for k, i in enumerate(y_others):
            remote(
                ys.at[p, rows_at(i, yrows)], y_recv.at[p, k], ys_send.at[p], ys_recv.at[p], at_y(i)
            ).start()

    @pl.when(even)
    def _():
        arrived(gb_recv, g_recv.at[0])
        gw[0] = gw[0] + gb_recv[...].astype(F32)

    for p in range(pieces):
        total = ys[p, rows_at(y, yrows), :].astype(F32)
        arrived(y_recv.at[p], ys_recv.at[p])
        for k in range(NY - 1):
            total = total + y_recv[p, k].astype(F32)
        z_all[p, 0] = total
        for k, i in enumerate(z_others):
            remote(
                z_all.at[p, 0], z_all.at[p, k + 1], zs_send.at[p], zs_recv.at[p], at_z(i)
            ).start()

    @pl.when(even)
    def _():
        arrived(gs_recv, g_recv.at[2])
        gs[...] += gs_recv[...].astype(F32)

    gs_copy = pltpu.make_async_copy(gs, gs_out, out_sem.at[0])
    gs_copy.start()
    arrived(gh_recv, g_recv.at[3])
    gw[0] = gw[0] + gh_recv[...].astype(F32)
    gd_copy = pltpu.make_async_copy(gw.at[0], gd_out, out_sem.at[1])
    gd_copy.start()

    for p in range(pieces):
        arrived(z_all.at[p, pl.ds(1, nz - 1)], zs_recv.at[p])
        total = z_all[p, z]
        for i in range(1, nz):
            total = total + z_all[p, lax.rem(z + nz - i, nz)]
        piece = rel_own.at[p, x, y]
        piece[...] = total.astype(BF16)
        for i in y_others:
            remote(piece, piece, ya_send.at[p], ya_recv.at[p], at_y(i)).start()

    for p in range(pieces):
        arrived(rel_own.at[p, x, pl.ds(0, NY - 1)], ya_recv.at[p])
        piece = rel_own.at[p, x]
        for i in x_others:
            remote(piece, piece, xa_send.at[p], xa_recv.at[p], at_x(i)).start()
    for p in range(pieces):
        arrived(rel_own.at[p, pl.ds(0, NX - 1)], xa_recv.at[p])
        remote(rel_own.at[p], rel_out.at[core, p], ca_send.at[p], ca_recv.at[p], sib).start()
        pltpu.make_async_copy(rel_own.at[p], rel_out.at[core, p], out_sem.at[2]).start()

    for copy in sent:
        copy.wait_send()

    @pl.when(even)
    def _():
        send_sib.wait_send()
        for copy in far[:2]:
            copy.wait_send()
        arrived(idx, far_send.at[2])
        src_copy.wait_send()

    @pl.when(core == 1)
    def _():
        home_copy.wait_send()

    for p in range(pieces):
        arrived(x_recv.at[p], xs_send.at[p])
        arrived(y_recv.at[p], ys_send.at[p])
        arrived(z_all.at[p, pl.ds(1, nz - 1)], zs_send.at[p])
        arrived(rel_own.at[p, x, pl.ds(0, NY - 1)], ya_send.at[p])
        arrived(rel_own.at[p, pl.ds(0, NX - 1)], xa_send.at[p])
        arrived(rel_own.at[p], ca_send.at[p])
    gs_copy.wait()
    gd_copy.wait()
    arrived(rel_own, out_sem.at[2])
    for p in range(pieces):
        arrived(rel_out.at[1 - core, p], ca_recv.at[p])


def store_kernel(
    rels, gs_in, gd_in, rel_in, gs_out, gd_out, rel_out, rel_b, rel_f, gs_v, gd_v, in_sem, out_sem
):
    ins = [
        pltpu.make_async_copy(rel_in, rel_b, in_sem.at[0]),
        pltpu.make_async_copy(gs_in, gs_v, in_sem.at[1]),
        pltpu.make_async_copy(gd_in, gd_v, in_sem.at[2]),
    ]
    outs = [
        pltpu.make_async_copy(rel_f, rel_out, out_sem.at[0]),
        pltpu.make_async_copy(gs_v, gs_out, out_sem.at[1]),
        pltpu.make_async_copy(gd_v, gd_out, out_sem.at[2]),
    ]
    for copy in ins:
        copy.start()
    half = rel_b.shape[2]
    ins[0].wait()
    for h in range(2):
        rel_f[:, h * half:(h + 1) * half] = rel_b[h, 0:rels, :].astype(F32)
    outs[0].start()
    for k in (1, 2):
        ins[k].wait()
        outs[k].start()
    for copy in outs:
        copy.wait()


def body(src_embed, dst_embed, relation, src_index, dst_index, rel_index, neg_index, edge_count):
    ent, width = src_embed.shape
    rels = relation.shape[0]
    steps = src_index.shape[2]
    nz = lax.axis_size("grp") // NX * ZLO
    half = width // 2
    pieces = -(-rels // (NX * NY * CHUNK))
    rows_mm = -(-rels // 128) * 128
    xrows = NY * CHUNK
    prows = NX * xrows
    tables = [t.reshape(steps, ent) for t in (src_index, dst_index, rel_index, neg_index)]
    vmem = pltpu.VMEM
    dma = pltpu.SemaphoreType.DMA
    block = vmem((ent, width), BF16)
    scratch = [
        vmem((4, ent, width), BF16),
        block,
        block,
        vmem((rels, width), F32),
        vmem((rows_mm, width), F32),
        vmem((2 * width, rows_mm), BF16),
        vmem((width, ent), BF16),
        vmem((4, steps, ent), jnp.int32),
        vmem((4, steps, ent), jnp.int32),
        vmem((1, steps), jnp.int32),
        vmem((1, steps), jnp.int32),
        vmem((4, ent, ent), BF16),
        vmem((4, rows_mm, ent), BF16),
        vmem((4, width, ent), BF16),
        vmem((4, width, ent), F32),
        vmem((4, width, ent), BF16),
        vmem((4, ent, 1), F32),
        vmem((4, ent, ent), BF16),
        vmem((4, width, ent), BF16),
        vmem((4, ent, width), F32),
        vmem((ent, width), F32),
        vmem((2, pieces * prows, half), F32),
        block, block, block, block, block, block, block, block,
        vmem((pieces, prows, half), F32),
        vmem((pieces, prows, half), BF16),
        vmem((pieces, NX - 1, xrows, half), BF16),
        vmem((pieces, xrows, half), BF16),
        vmem((pieces, NY - 1, CHUNK, half), BF16),
        vmem((pieces, nz, CHUNK, half), F32),
        vmem((pieces, NX, NY, CHUNK, half), BF16),
        dma((5,)),
        dma((3,)),
        dma((3,)),
        dma((4,)),
        dma((3,)), dma((3,)),
        dma((4,)), dma((4,)),
    ] + [dma((pieces,))] * 14
    anywhere = pl.BlockSpec(memory_space=pl.ANY)
    grad = jax.ShapeDtypeStruct((ent, width), F32)
    grad_src, grad_dst, rel_parts = pl.pallas_call(
        functools.partial(kernel, nz, rels, rows_mm, pieces),
        out_shape=(
            grad, grad, jax.ShapeDtypeStruct((2, pieces, NX, NY, CHUNK, half), BF16)
        ),
        in_specs=[anywhere] * 8,
        out_specs=(anywhere,) * 3,
        scratch_shapes=scratch,
        compiler_params=pltpu.CompilerParams(
            collective_id=0, has_side_effects=True, vmem_limit_bytes=56 * 1024 * 1024
        ),
    )(src_embed, dst_embed, relation, *tables, edge_count.reshape(1, steps))
    rel_parts = rel_parts.reshape(2, pieces * prows, half)
    return pl.pallas_call(
        functools.partial(store_kernel, rels),
        out_shape=(grad, grad, jax.ShapeDtypeStruct((rels, width), F32)),
        in_specs=[anywhere] * 3,
        out_specs=(anywhere,) * 3,
        scratch_shapes=[
            vmem(rel_parts.shape, BF16), vmem((rels, width), F32),
            vmem((ent, width), F32), vmem((ent, width), F32), dma((3,)), dma((3,)),
        ],
        compiler_params=pltpu.CompilerParams(vmem_limit_bytes=56 * 1024 * 1024),
    )(grad_src, grad_dst, rel_parts)


def solution(mesh):
    in_specs = (
        P(("grp", "blk"), None),
        P(("grp", "blk"), None),
        P(),
        P("grp", "blk", None, None),
        P("grp", "blk", None, None),
        P("grp", "blk", None, None),
        P("grp", "blk", None, None),
        P("grp", "blk", None),
    )
    out_specs = (P(("grp", "blk"), None), P(("grp", "blk"), None), P())
    return jax.shard_map(body, mesh=mesh, in_specs=in_specs, out_specs=out_specs, check_vma=False)
```

```python
import functools

import jax
import jax.numpy as jnp
from jax import lax
from jax.experimental import pallas as pl
from jax.experimental.pallas import tpu as pltpu
from jax.sharding import PartitionSpec as P

MESH = pl.DeviceIdType.MESH
F32 = jnp.float32
BF16 = jnp.bfloat16
NX = 4
NY = 8
ZLO = 2
CHUNK = 16
STEP = 128


def nt(a, b):
    return lax.dot_general(a, b, (((1,), (1,)), ((), ())), preferred_element_type=F32)


def nn(a, b):
    return jnp.dot(a, b, preferred_element_type=F32)


def kernel(
    nz, rels, rows_mm, pieces,
    src_hbm, dst_hbm, rel_hbm, si_hbm, di_hbm, ri_hbm, ni_hbm, ec_hbm,
    gs_out, gd_out, rel_out,
    part, src_v, src_far, rel_v, rel_pad, rel_t, src_t, idx, idx_far, ec, ec_far,
    ohs, ohr, sr, rr, qt, weight, pulls, back_v, value, gw, gs, gr,
    gs_send, gs_recv, ga_send, ga_recv, gb_send, gb_recv, gh_send, gh_recv,
    half_recv, xs, x_recv, ys, y_recv, z_all, rel_own,
    in_sem, out_sem, part_send, part_recv, far_send, far_recv,
    g_send, g_recv, s_send, s_recv,
    xs_send, xs_recv, ys_send, ys_recv, zs_send, zs_recv,
    ya_send, ya_recv, xa_send, xa_recv, ca_send, ca_recv,
):
    ent, width = dst_hbm.shape
    half = width // 2
    yrows = CHUNK
    xrows = NY * yrows
    prows = NX * xrows
    nchip = ZLO * NY
    grp, blk = lax.axis_index("grp"), lax.axis_index("blk")
    core = lax.rem(blk, 2)
    chip = blk // 2
    y = lax.rem(chip, NY)
    z = (grp // NX) * ZLO + chip // NY
    x = lax.rem(grp, NX)
    even = core == 0
    nxt = lax.rem(chip + 1, nchip) * 2 + core
    prv = lax.rem(chip + nchip - 1, nchip) * 2 + core
    sib = (grp, chip * 2 + 1 - core)

    def at_x(i):
        return ((grp // NX) * NX + i, blk)

    def at_y(i):
        return (grp, (chip // NY) * NY * 2 + i * 2 + core)

    def at_z(i):
        return ((i // ZLO) * NX + x, lax.rem(i, ZLO) * NY * 2 + y * 2 + core)

    x_others = [lax.rem(x + k, NX) for k in range(1, NX)]
    y_others = [lax.rem(y + k, NY) for k in range(1, NY)]
    z_others = [lax.rem(z + k, nz) for k in range(1, nz)]

    def remote(source, target, send, recv, device):
        return pltpu.make_async_remote_copy(
            src_ref=source, dst_ref=target, send_sem=send, recv_sem=recv,
            device_id=device, device_id_type=MESH,
        )

    def arrived(buffer, recv):
        pltpu.make_async_copy(buffer, buffer, recv).wait()

    own = [(si_hbm, 0), (di_hbm, 1), (ri_hbm, 2), (ni_hbm, 3)]
    loads = [
        pltpu.make_async_copy(ec_hbm, ec, in_sem.at[3]),
        pltpu.make_async_copy(rel_hbm, rel_v, in_sem.at[0]),
        pltpu.make_async_copy(src_hbm, src_v, in_sem.at[1]),
        pltpu.make_async_copy(dst_hbm, part.at[0], in_sem.at[2]),
    ]
    for load in [pltpu.make_async_copy(ref, idx.at[k], in_sem.at[4]) for ref, k in own] + loads:
        load.start()
    barrier = pltpu.get_barrier_semaphore()
    greet = [sib, (grp, nxt), (grp, prv)]
    greet += [at_x(i) for i in x_others] + [at_y(i) for i in y_others] + [at_z(i) for i in z_others]
    for device in greet:
        pl.semaphore_signal(barrier, inc=1, device_id=device, device_id_type=MESH)
    if rows_mm < pieces * prows:
        gr[:, rows_mm:, :] = jnp.zeros((2, pieces * prows - rows_mm, half), F32)
    tail = rels // 8 * 8
    rel_pad[tail:, :] = jnp.zeros((rows_mm - tail, width), F32)

    def tile_of(w):
        if w in (0, 3):
            return w
        return jnp.where(even, 3 - w, w)

    def row_of(k, w):
        row = idx[k, pl.ds(tile_of(w), 1), :]
        if w == 3:
            row = jnp.where(even, idx_far[k, 3:4, :], row)
        return row

    def live_of(w):
        counts = ec[...].astype(F32)
        if w == 3:
            counts = jnp.where(even, ec_far[...].astype(F32), counts)
        place = lax.broadcasted_iota(jnp.int32, counts.shape, 1)
        count = jnp.sum(jnp.where(place == tile_of(w), counts, 0.0), axis=1, keepdims=True)
        slot = lax.broadcasted_iota(jnp.int32, (1, ent), 1).astype(F32)
        return slot < count

    def lanes(w):
        return pl.ds(w * ent, ent)

    def tables(w):
        rows = lax.broadcasted_iota(jnp.int32, (ent, ent), 0)
        ohs[:, lanes(w)] = (rows == jnp.where(live_of(w), row_of(0, w), -1)).astype(BF16)
        chosen = (rows == row_of(3, w)).astype(F32)
        weight[w] = jnp.sum(chosen, axis=1, keepdims=True) * (1.0 / ent)
        rows = lax.broadcasted_iota(jnp.int32, (rows_mm, ent), 0)
        ohr[:, lanes(w)] = (rows == row_of(2, w)).astype(BF16)

    def gather(w):
        picked = nn(src_t[...], ohs[:, lanes(w)])
        both = nn(rel_t[...], ohr[:, lanes(w)])
        scale = both[0:width] + both[width:]
        sr[w] = picked.astype(BF16)
        rr[w] = scale
        qt[w] = (picked * scale).astype(BF16)

    def finish(w, slot):
        block = part[slot]
        for low in range(0, ent, STEP):
            scores = nn(block[low:low + STEP], qt[w])
            rows = low + lax.broadcasted_iota(jnp.int32, (STEP, ent), 0)
            decay = jnp.exp(jnp.minimum(-scores, 87.0))
            share = weight[w, low:low + STEP]
            share = jnp.where(rows == row_of(1, w), share - decay, share)
            pulls[w, low:low + STEP] = (pl.reciprocal(1.0 + decay, approx=True) * share).astype(BF16)
        pull = pulls[w]
        dquery = nn(block.T, pull)
        back_v[:, lanes(w)] = (dquery * rr[w]).astype(BF16)
        value[:, lanes(w)] = (dquery * sr[w].astype(F32)).astype(BF16)

    def grow(p, first, last):
        low, high = p * prows, min((p + 1) * prows, rows_mm)
        span = pl.ds(first * ent, (last - first) * ent)
        grown = nt(ohr[low:high, span], value[:, span])
        for h in range(2):
            grown_half = grown[:, h * half:(h + 1) * half]
            if first == 0:
                gr[h, low:high, :] = grown_half
            else:
                gr[h, low:high, :] += grown_half

    swaps = [
        remote(
            gr.at[1 - core, pl.ds(p * prows, prows)], half_recv.at[p],
            s_send.at[p], s_recv.at[p], sib,
        )
        for p in range(pieces)
    ]

    arrived(idx, in_sem.at[4])
    loads[0].wait()
    for w in range(3):
        tables(w)

    pl.semaphore_wait(barrier, len(greet))

    direct = 2 - core
    send_next = remote(
        dst_hbm, part.at[direct], part_send.at[0], part_recv.at[direct], (grp, nxt)
    )
    send_next.start()
    send_sib = remote(dst_hbm, part.at[3], part_send.at[1], part_recv.at[3], sib)
    far = [remote(src_hbm, src_far, far_send.at[0], far_recv.at[0], (grp, prv))]
    far += [remote(ec_hbm, ec_far, far_send.at[1], far_recv.at[1], (grp, prv))]
    far += [
        remote(ref, idx_far.at[k], far_send.at[2], far_recv.at[2], (grp, prv))
        for ref, k in own
    ]

    @pl.when(even)
    def _():
        send_sib.start()
        for copy in far:
            copy.start()

    for load in loads[1:]:
        load.wait()
    rel_pad[0:rels, :] = rel_v[...]
    turned = rel_pad[...].T
    high = turned.astype(BF16)
    rel_t[0:width, :] = high
    rel_t[width:, :] = (turned - high.astype(F32)).astype(BF16)
    src_t[...] = src_v[...].T

    gather(0)
    finish(0, 0)
    for p in range(pieces):
        grow(p, 0, 1)
    gather(1)
    gather(2)

    @pl.when(even)
    def _():
        arrived(idx_far, far_recv.at[2])
        arrived(ec_far, far_recv.at[1])
        arrived(src_far, far_recv.at[0])
        src_t[...] = src_far[...].T

    tables(3)
    gather(3)

    arrived(part.at[direct], part_recv.at[direct])
    forward = remote(
        part.at[direct], part.at[direct], part_send.at[2], part_recv.at[direct], sib
    )
    forward.start()

    @pl.when(core == 1)
    def _():
        arrived(part.at[3], part_recv.at[3])

    finish(1, 2 + core)
    other = 1 + core
    arrived(part.at[other], part_recv.at[other])
    finish(2, 1)
    finish(3, 1 + core)
    for p in range(pieces):
        grow(p, 1, 4)
        swaps[p].start()

    sent = [send_next, forward] + swaps

    def rows_at(i, size):
        return pl.ds(pl.multiple_of(i * size, size), size)

    for w in range(3):
        gw[w] = nt(pulls[w], qt[w])
    for p in range(pieces):
        arrived(half_recv.at[p], s_recv.at[p])
        xs[p] = (gr[core, p * prows:(p + 1) * prows, :] + half_recv[p]).astype(BF16)
        for k, i in enumerate(x_others):
            remote(
                xs.at[p, rows_at(i, xrows)], x_recv.at[p, k], xs_send.at[p], xs_recv.at[p], at_x(i)
            ).start()

    own_slots = pl.ds(0, 3 * ent)
    gs[...] = nt(ohs[:, own_slots], back_v[:, own_slots])
    last = nt(ohs[:, lanes(3)], back_v[:, lanes(3)])
    gw[3] = nt(pulls[3], qt[3])
    ga_send[...] = (gw[3] + jnp.where(even, gw[2], 0.0)).astype(BF16)
    pair_copy = remote(ga_send, ga_recv, g_send.at[1], g_recv.at[1], sib)
    pair_copy.start()
    gs_send[...] = last.astype(BF16)
    src_copy = remote(gs_send, gs_recv, g_send.at[2], g_recv.at[2], (grp, nxt))
    gb_send[...] = gw[1].astype(BF16)
    home_copy = remote(gb_send, gb_recv, g_send.at[0], g_recv.at[0], sib)

    @pl.when(even)
    def _():
        src_copy.start()

    @pl.when(core == 1)
    def _():
        home_copy.start()
        gs[...] += last

    arrived(ga_recv, g_recv.at[1])
    gh_send[...] = (gw[1 + core] + ga_recv[...].astype(F32)).astype(BF16)
    homeward = remote(gh_send, gh_recv, g_send.at[3], g_recv.at[3], (grp, prv))
    homeward.start()
    sent += [pair_copy, homeward]

    for p in range(pieces):
        total = xs[p, rows_at(x, xrows), :].astype(F32)
        arrived(x_recv.at[p], xs_recv.at[p])
        for k in range(NX - 1):
            total = total + x_recv[p, k].astype(F32)
        ys[p] = total.astype(BF16)
        for k, i in enumerate(y_others):
            remote(
                ys.at[p, rows_at(i, yrows)], y_recv.at[p, k], ys_send.at[p], ys_recv.at[p], at_y(i)
            ).start()

    @pl.when(even)
    def _():
        arrived(gb_recv, g_recv.at[0])
        gw[0] = gw[0] + gb_recv[...].astype(F32)

    for p in range(pieces):
        total = ys[p, rows_at(y, yrows), :].astype(F32)
        arrived(y_recv.at[p], ys_recv.at[p])
        for k in range(NY - 1):
            total = total + y_recv[p, k].astype(F32)
        z_all[p, 0] = total
        for k, i in enumerate(z_others):
            remote(
                z_all.at[p, 0], z_all.at[p, k + 1], zs_send.at[p], zs_recv.at[p], at_z(i)
            ).start()

    @pl.when(even)
    def _():
        arrived(gs_recv, g_recv.at[2])
        gs[...] += gs_recv[...].astype(F32)

    gs_copy = pltpu.make_async_copy(gs, gs_out, out_sem.at[0])
    gs_copy.start()
    arrived(gh_recv, g_recv.at[3])
    gw[0] = gw[0] + gh_recv[...].astype(F32)
    gd_copy = pltpu.make_async_copy(gw.at[0], gd_out, out_sem.at[1])
    gd_copy.start()

    for p in range(pieces):
        arrived(z_all.at[p, pl.ds(1, nz - 1)], zs_recv.at[p])
        total = z_all[p, z]
        for i in range(1, nz):
            total = total + z_all[p, lax.rem(z + nz - i, nz)]
        piece = rel_own.at[p, x, y]
        piece[...] = total.astype(BF16)
        for i in y_others:
            remote(piece, piece, ya_send.at[p], ya_recv.at[p], at_y(i)).start()

    for p in range(pieces):
        arrived(rel_own.at[p, x, pl.ds(0, NY - 1)], ya_recv.at[p])
        piece = rel_own.at[p, x]
        for i in x_others:
            remote(piece, piece, xa_send.at[p], xa_recv.at[p], at_x(i)).start()
    for p in range(pieces):
        arrived(rel_own.at[p, pl.ds(0, NX - 1)], xa_recv.at[p])
        remote(rel_own.at[p], rel_out.at[core, p], ca_send.at[p], ca_recv.at[p], sib).start()
        pltpu.make_async_copy(rel_own.at[p], rel_out.at[core, p], out_sem.at[2]).start()

    for copy in sent:
        copy.wait_send()

    @pl.when(even)
    def _():
        send_sib.wait_send()
        for copy in far[:2]:
            copy.wait_send()
        arrived(idx, far_send.at[2])
        src_copy.wait_send()

    @pl.when(core == 1)
    def _():
        home_copy.wait_send()

    for p in range(pieces):
        arrived(x_recv.at[p], xs_send.at[p])
        arrived(y_recv.at[p], ys_send.at[p])
        arrived(z_all.at[p, pl.ds(1, nz - 1)], zs_send.at[p])
        arrived(rel_own.at[p, x, pl.ds(0, NY - 1)], ya_send.at[p])
        arrived(rel_own.at[p, pl.ds(0, NX - 1)], xa_send.at[p])
        arrived(rel_own.at[p], ca_send.at[p])
    gs_copy.wait()
    gd_copy.wait()
    arrived(rel_own, out_sem.at[2])
    for p in range(pieces):
        arrived(rel_out.at[1 - core, p], ca_recv.at[p])


def store_kernel(
    rels, gs_in, gd_in, rel_in, gs_out, gd_out, rel_out, rel_b, rel_f, gs_v, gd_v, in_sem, out_sem
):
    loads = [
        pltpu.make_async_copy(rel_in, rel_b, in_sem.at[0]),
        pltpu.make_async_copy(gs_in, gs_v, in_sem.at[1]),
        pltpu.make_async_copy(gd_in, gd_v, in_sem.at[2]),
    ]
    stores = [
        pltpu.make_async_copy(rel_f, rel_out, out_sem.at[0]),
        pltpu.make_async_copy(gs_v, gs_out, out_sem.at[1]),
        pltpu.make_async_copy(gd_v, gd_out, out_sem.at[2]),
    ]
    for load in loads:
        load.start()
    half = rel_b.shape[2]
    loads[0].wait()
    for h in range(2):
        rel_f[:, h * half:(h + 1) * half] = rel_b[h, 0:rels, :].astype(F32)
    stores[0].start()
    for k in (1, 2):
        loads[k].wait()
        stores[k].start()
    for store in stores:
        store.wait()


def body(src_embed, dst_embed, relation, src_index, dst_index, rel_index, neg_index, edge_count):
    ent, width = src_embed.shape
    rels = relation.shape[0]
    steps = src_index.shape[2]
    nz = lax.axis_size("grp") // NX * ZLO
    half = width // 2
    pieces = -(-rels // (NX * NY * CHUNK))
    rows_mm = -(-rels // 128) * 128
    xrows = NY * CHUNK
    prows = NX * xrows
    tables = [t.reshape(steps, ent) for t in (src_index, dst_index, rel_index, neg_index)]
    vmem = pltpu.VMEM
    dma = pltpu.SemaphoreType.DMA
    block = vmem((ent, width), BF16)
    scratch = [
        vmem((4, ent, width), BF16),
        block,
        block,
        vmem((rels, width), F32),
        vmem((rows_mm, width), F32),
        vmem((2 * width, rows_mm), BF16),
        vmem((width, ent), BF16),
        vmem((4, steps, ent), jnp.int32),
        vmem((4, steps, ent), jnp.int32),
        vmem((1, steps), jnp.int32),
        vmem((1, steps), jnp.int32),
        vmem((ent, 4 * ent), BF16),
        vmem((rows_mm, 4 * ent), BF16),
        vmem((4, width, ent), BF16),
        vmem((4, width, ent), F32),
        vmem((4, width, ent), BF16),
        vmem((4, ent, 1), F32),
        vmem((4, ent, ent), BF16),
        vmem((width, 4 * ent), BF16),
        vmem((width, 4 * ent), BF16),
        vmem((4, ent, width), F32),
        vmem((ent, width), F32),
        vmem((2, pieces * prows, half), F32),
        block, block, block, block, block, block, block, block,
        vmem((pieces, prows, half), F32),
        vmem((pieces, prows, half), BF16),
        vmem((pieces, NX - 1, xrows, half), BF16),
        vmem((pieces, xrows, half), BF16),
        vmem((pieces, NY - 1, CHUNK, half), BF16),
        vmem((pieces, nz, CHUNK, half), F32),
        vmem((pieces, NX, NY, CHUNK, half), BF16),
        dma((5,)),
        dma((3,)),
        dma((3,)),
        dma((4,)),
        dma((3,)), dma((3,)),
        dma((4,)), dma((4,)),
    ] + [dma((pieces,))] * 14
    anywhere = pl.BlockSpec(memory_space=pl.ANY)
    grad = jax.ShapeDtypeStruct((ent, width), F32)
    grad_src, grad_dst, rel_parts = pl.pallas_call(
        functools.partial(kernel, nz, rels, rows_mm, pieces),
        out_shape=(
            grad, grad, jax.ShapeDtypeStruct((2, pieces, NX, NY, CHUNK, half), BF16)
        ),
        in_specs=[anywhere] * 8,
        out_specs=(anywhere,) * 3,
        scratch_shapes=scratch,
        compiler_params=pltpu.CompilerParams(
            collective_id=0, has_side_effects=True, vmem_limit_bytes=56 * 1024 * 1024
        ),
    )(src_embed, dst_embed, relation, *tables, edge_count.reshape(1, steps))
    rel_parts = rel_parts.reshape(2, pieces * prows, half)
    return pl.pallas_call(
        functools.partial(store_kernel, rels),
        out_shape=(grad, grad, jax.ShapeDtypeStruct((rels, width), F32)),
        in_specs=[anywhere] * 3,
        out_specs=(anywhere,) * 3,
        scratch_shapes=[
            vmem(rel_parts.shape, BF16), vmem((rels, width), F32),
            vmem((ent, width), F32), vmem((ent, width), F32), dma((3,)), dma((3,)),
        ],
        compiler_params=pltpu.CompilerParams(vmem_limit_bytes=56 * 1024 * 1024),
    )(grad_src, grad_dst, rel_parts)


def solution(mesh):
    in_specs = (
        P(("grp", "blk"), None),
        P(("grp", "blk"), None),
        P(),
        P("grp", "blk", None, None),
        P("grp", "blk", None, None),
        P("grp", "blk", None, None),
        P("grp", "blk", None, None),
        P("grp", "blk", None),
    )
    out_specs = (P(("grp", "blk"), None), P(("grp", "blk"), None), P())
    return jax.shard_map(body, mesh=mesh, in_specs=in_specs, out_specs=out_specs, check_vma=False)
```

```python
import functools

import jax
import jax.numpy as jnp
from jax import lax
from jax.experimental import pallas as pl
from jax.experimental.pallas import tpu as pltpu
from jax.sharding import PartitionSpec as P

MESH = pl.DeviceIdType.MESH
F32 = jnp.float32
BF16 = jnp.bfloat16
NX = 4
NY = 8
ZLO = 2
CHUNK = 16
STEP = 128


def nt(a, b):
    return lax.dot_general(a, b, (((1,), (1,)), ((), ())), preferred_element_type=F32)


def nn(a, b):
    return jnp.dot(a, b, preferred_element_type=F32)


def kernel(
    nz, rels, rows_mm, pieces,
    src_hbm, dst_hbm, rel_hbm, si_hbm, di_hbm, ri_hbm, ni_hbm, ec_hbm,
    gs_out, gd_out, rel_out,
    part, src_v, src_far, rel_v, rel_pad, rel_t, src_t, idx, idx_far, ec, ec_far,
    ohs, ohr, sr, rr, qt, weight, pulls, back_v, value, gw, gs, gr,
    gs_send, gs_recv, ga_send, ga_recv, gb_send, gb_recv, gh_send, gh_recv,
    half_recv, xs, x_recv, ys, y_recv, z_all, rel_own,
    in_sem, out_sem, part_send, part_recv, far_send, far_recv,
    g_send, g_recv, s_send, s_recv,
    xs_send, xs_recv, ys_send, ys_recv, zs_send, zs_recv,
    ya_send, ya_recv, xa_send, xa_recv, ca_send, ca_recv,
):
    ent, width = dst_hbm.shape
    half = width // 2
    yrows = CHUNK
    xrows = NY * yrows
    prows = NX * xrows
    nchip = ZLO * NY
    grp, blk = lax.axis_index("grp"), lax.axis_index("blk")
    core = lax.rem(blk, 2)
    chip = blk // 2
    y = lax.rem(chip, NY)
    z = (grp // NX) * ZLO + chip // NY
    x = lax.rem(grp, NX)
    even = core == 0
    nxt = lax.rem(chip + 1, nchip) * 2 + core
    prv = lax.rem(chip + nchip - 1, nchip) * 2 + core
    sib = (grp, chip * 2 + 1 - core)

    def at_x(i):
        return ((grp // NX) * NX + i, blk)

    def at_y(i):
        return (grp, (chip // NY) * NY * 2 + i * 2 + core)

    def at_z(i):
        return ((i // ZLO) * NX + x, lax.rem(i, ZLO) * NY * 2 + y * 2 + core)

    def ring(place, size):
        steps = sorted(range(1, size), key=lambda k: -min(k, size - k))
        return [(k, lax.rem(place + k, size)) for k in steps]

    x_others, y_others, z_others = ring(x, NX), ring(y, NY), ring(z, nz)

    def remote(source, target, send, recv, device):
        return pltpu.make_async_remote_copy(
            src_ref=source, dst_ref=target, send_sem=send, recv_sem=recv,
            device_id=device, device_id_type=MESH,
        )

    def arrived(buffer, recv):
        pltpu.make_async_copy(buffer, buffer, recv).wait()

    own = [(si_hbm, 0), (di_hbm, 1), (ri_hbm, 2), (ni_hbm, 3)]
    loads = [
        pltpu.make_async_copy(ec_hbm, ec, in_sem.at[3]),
        pltpu.make_async_copy(dst_hbm, part.at[0], in_sem.at[2]),
        pltpu.make_async_copy(src_hbm, src_v, in_sem.at[1]),
        pltpu.make_async_copy(rel_hbm, rel_v, in_sem.at[0]),
    ]
    tables_in = [pltpu.make_async_copy(ref, idx.at[k], in_sem.at[4]) for ref, k in own]
    for load in loads[:2] + tables_in + loads[2:]:
        load.start()
    barrier = pltpu.get_barrier_semaphore()
    greet = [sib, (grp, nxt), (grp, prv)]
    greet += [at_x(i) for _, i in x_others] + [at_y(i) for _, i in y_others]
    greet += [at_z(i) for _, i in z_others]
    for device in greet:
        pl.semaphore_signal(barrier, inc=1, device_id=device, device_id_type=MESH)
    if rows_mm < pieces * prows:
        gr[:, rows_mm:, :] = jnp.zeros((2, pieces * prows - rows_mm, half), F32)
    tail = rels // 8 * 8
    rel_pad[tail:, :] = jnp.zeros((rows_mm - tail, width), F32)

    def tile_of(w):
        if w in (0, 3):
            return w
        return jnp.where(even, 3 - w, w)

    def row_of(k, w):
        row = idx[k, pl.ds(tile_of(w), 1), :]
        if w == 3:
            row = jnp.where(even, idx_far[k, 3:4, :], row)
        return row

    def live_of(w):
        counts = ec[...].astype(F32)
        if w == 3:
            counts = jnp.where(even, ec_far[...].astype(F32), counts)
        place = lax.broadcasted_iota(jnp.int32, counts.shape, 1)
        count = jnp.sum(jnp.where(place == tile_of(w), counts, 0.0), axis=1, keepdims=True)
        slot = lax.broadcasted_iota(jnp.int32, (1, ent), 1).astype(F32)
        return slot < count

    def lanes(w):
        return pl.ds(w * ent, ent)

    def tables(w):
        rows = lax.broadcasted_iota(jnp.int32, (ent, ent), 0)
        ohs[:, lanes(w)] = (rows == jnp.where(live_of(w), row_of(0, w), -1)).astype(BF16)
        chosen = (rows == row_of(3, w)).astype(F32)
        weight[w] = jnp.sum(chosen, axis=1, keepdims=True) * (1.0 / ent)
        rows = lax.broadcasted_iota(jnp.int32, (rows_mm, ent), 0)
        ohr[:, lanes(w)] = (rows == row_of(2, w)).astype(BF16)

    def gather(w):
        picked = nn(src_t[...], ohs[:, lanes(w)])
        both = nn(rel_t[...], ohr[:, lanes(w)])
        scale = both[0:width] + both[width:]
        sr[w] = picked.astype(BF16)
        rr[w] = scale
        qt[w] = (picked * scale).astype(BF16)

    def score(w, slot, h):
        mid = ent // 2
        for low in range(h * mid, (h + 1) * mid, min(STEP, mid)):
            size = min(STEP, mid)
            scores = nn(part[slot, low:low + size, :], qt[w])
            rows = low + lax.broadcasted_iota(jnp.int32, (size, ent), 0)
            decay = jnp.exp(jnp.minimum(-scores, 87.0))
            share = weight[w, low:low + size]
            share = jnp.where(rows == row_of(1, w), share - decay, share)
            inverse = pl.reciprocal(1.0 + decay, approx=True)
            pulls[w, low:low + size] = (inverse * share).astype(BF16)

    def pull_half(w, slot, h):
        return nn(part[slot, halves[h], :].T, pulls[w, halves[h], :])

    def give(w, dquery):
        back_v[:, lanes(w)] = (dquery * rr[w]).astype(BF16)
        value[:, lanes(w)] = (dquery * sr[w].astype(F32)).astype(BF16)

    def finish(w, slot):
        score(w, slot, 0)
        score(w, slot, 1)
        give(w, nn(part[slot].T, pulls[w]))

    def grow(p, first, last):
        low, high = p * prows, min((p + 1) * prows, rows_mm)
        span = pl.ds(first * ent, (last - first) * ent)
        grown = nt(ohr[low:high, span], value[:, span])
        for h in range(2):
            grown_half = grown[:, h * half:(h + 1) * half]
            if first == 0:
                gr[h, low:high, :] = grown_half
            else:
                gr[h, low:high, :] += grown_half

    swaps = [
        remote(
            gr.at[1 - core, pl.ds(p * prows, prows)], half_recv.at[p],
            s_send.at[p], s_recv.at[p], sib,
        )
        for p in range(pieces)
    ]

    arrived(idx, in_sem.at[4])
    loads[0].wait()
    for w in range(3):
        tables(w)

    pl.semaphore_wait(barrier, len(greet))

    direct = 2 - core
    other = 1 + core
    halves = [pl.ds(0, ent // 2), pl.ds(ent // 2, ent // 2)]

    def send_part(source, slot, h, send, device):
        return remote(
            source.at[halves[h]], part.at[slot, halves[h]], part_send.at[send, h],
            part_recv.at[slot, h], device,
        )

    def arrived_part(slot, h):
        arrived(part.at[slot, halves[h]], part_recv.at[slot, h])

    send_next = [send_part(part.at[0], direct, h, 0, (grp, nxt)) for h in range(2)]
    send_sib = [send_part(part.at[0], 3, h, 1, sib) for h in range(2)]
    forward = [send_part(part.at[direct], direct, h, 2, sib) for h in range(2)]
    loads[1].wait()
    for copy in send_next:
        copy.start()
    far = [remote(src_hbm, src_far, far_send.at[0], far_recv.at[0], (grp, prv))]
    far += [remote(ec_hbm, ec_far, far_send.at[1], far_recv.at[1], (grp, prv))]
    far += [
        remote(ref, idx_far.at[k], far_send.at[2], far_recv.at[2], (grp, prv))
        for ref, k in own
    ]

    @pl.when(even)
    def _():
        for copy in send_sib + far:
            copy.start()

    for load in loads[2:]:
        load.wait()
    rel_pad[0:rels, :] = rel_v[...]
    turned = rel_pad[...].T
    high = turned.astype(BF16)
    rel_t[0:width, :] = high
    rel_t[width:, :] = (turned - high.astype(F32)).astype(BF16)
    src_t[...] = src_v[...].T

    gather(0)
    finish(0, 0)
    gather(1)
    gather(2)

    @pl.when(even)
    def _():
        arrived(idx_far, far_recv.at[2])
        arrived(ec_far, far_recv.at[1])
        arrived(src_far, far_recv.at[0])
        src_t[...] = src_far[...].T

    tables(3)
    gather(3)

    for h in range(2):
        arrived_part(direct, h)
        forward[h].start()

    @pl.when(core == 1)
    def _():
        arrived_part(3, 0)
        arrived_part(3, 1)

    finish(1, 2 + core)
    for p in range(pieces):
        grow(p, 0, 2)
    arrived_part(other, 0)
    score(2, 1, 0)
    score(3, other, 0)
    first = [pull_half(2, 1, 0), pull_half(3, other, 0)]
    arrived_part(other, 1)
    score(2, 1, 1)
    score(3, other, 1)
    give(2, first[0] + pull_half(2, 1, 1))
    give(3, first[1] + pull_half(3, other, 1))
    for p in range(pieces):
        grow(p, 2, 4)
        swaps[p].start()

    sent = send_next + forward + swaps

    def rows_at(i, size):
        return pl.ds(pl.multiple_of(i * size, size), size)

    for w in (2, 3):
        gw[w] = nt(pulls[w], qt[w])
    ga_send[...] = (gw[3] + jnp.where(even, gw[2], 0.0)).astype(BF16)
    pair_copy = remote(ga_send, ga_recv, g_send.at[1], g_recv.at[1], sib)
    pair_copy.start()
    last = nt(ohs[:, lanes(3)], back_v[:, lanes(3)])
    gs_send[...] = last.astype(BF16)
    src_copy = remote(gs_send, gs_recv, g_send.at[2], g_recv.at[2], (grp, nxt))

    @pl.when(even)
    def _():
        src_copy.start()

    gw[1] = nt(pulls[1], qt[1])
    gb_send[...] = gw[1].astype(BF16)
    home_copy = remote(gb_send, gb_recv, g_send.at[0], g_recv.at[0], sib)

    @pl.when(core == 1)
    def _():
        home_copy.start()

    for p in range(pieces):
        arrived(half_recv.at[p], s_recv.at[p])
        xs[p] = (gr[core, p * prows:(p + 1) * prows, :] + half_recv[p]).astype(BF16)
        for k, i in x_others:
            remote(
                xs.at[p, rows_at(i, xrows)], x_recv.at[p, k - 1], xs_send.at[p], xs_recv.at[p], at_x(i)
            ).start()

    arrived(ga_recv, g_recv.at[1])
    gh_send[...] = (gw[1 + core] + ga_recv[...].astype(F32)).astype(BF16)
    homeward = remote(gh_send, gh_recv, g_send.at[3], g_recv.at[3], (grp, prv))
    homeward.start()
    sent += [pair_copy, homeward]
    gw[0] = nt(pulls[0], qt[0])
    own_slots = pl.ds(0, 3 * ent)
    gs[...] = nt(ohs[:, own_slots], back_v[:, own_slots])

    @pl.when(core == 1)
    def _():
        gs[...] += last

    for p in range(pieces):
        total = xs[p, rows_at(x, xrows), :].astype(F32)
        arrived(x_recv.at[p], xs_recv.at[p])
        for k in range(NX - 1):
            total = total + x_recv[p, k].astype(F32)
        ys[p] = total.astype(BF16)
        for k, i in y_others:
            remote(
                ys.at[p, rows_at(i, yrows)], y_recv.at[p, k - 1], ys_send.at[p], ys_recv.at[p], at_y(i)
            ).start()

    for p in range(pieces):
        total = ys[p, rows_at(y, yrows), :].astype(F32)
        arrived(y_recv.at[p], ys_recv.at[p])
        for k in range(NY - 1):
            total = total + y_recv[p, k].astype(F32)
        z_all[p, 0] = total
        for k, i in z_others:
            remote(
                z_all.at[p, 0], z_all.at[p, k], zs_send.at[p], zs_recv.at[p], at_z(i)
            ).start()

    @pl.when(even)
    def _():
        arrived(gs_recv, g_recv.at[2])
        gs[...] += gs_recv[...].astype(F32)
        arrived(gb_recv, g_recv.at[0])
        gw[0] = gw[0] + gb_recv[...].astype(F32)

    gs_copy = pltpu.make_async_copy(gs, gs_out, out_sem.at[0])
    gs_copy.start()
    arrived(gh_recv, g_recv.at[3])
    gw[0] = gw[0] + gh_recv[...].astype(F32)
    gd_copy = pltpu.make_async_copy(gw.at[0], gd_out, out_sem.at[1])
    gd_copy.start()

    for p in range(pieces):
        arrived(z_all.at[p, pl.ds(1, nz - 1)], zs_recv.at[p])
        total = z_all[p, z]
        for i in range(1, nz):
            total = total + z_all[p, lax.rem(z + nz - i, nz)]
        piece = rel_own.at[p, x, y]
        piece[...] = total.astype(BF16)
        for _, i in y_others:
            remote(piece, piece, ya_send.at[p], ya_recv.at[p], at_y(i)).start()

    for p in range(pieces):
        arrived(rel_own.at[p, x, pl.ds(0, NY - 1)], ya_recv.at[p])
        piece = rel_own.at[p, x]
        for _, i in x_others:
            remote(piece, piece, xa_send.at[p], xa_recv.at[p], at_x(i)).start()
    for p in range(pieces):
        arrived(rel_own.at[p, pl.ds(0, NX - 1)], xa_recv.at[p])
        remote(rel_own.at[p], rel_out.at[core, p], ca_send.at[p], ca_recv.at[p], sib).start()
        pltpu.make_async_copy(rel_own.at[p], rel_out.at[core, p], out_sem.at[2]).start()

    for copy in sent:
        copy.wait_send()

    @pl.when(even)
    def _():
        for copy in send_sib + far[:2]:
            copy.wait_send()
        arrived(idx, far_send.at[2])
        src_copy.wait_send()

    @pl.when(core == 1)
    def _():
        home_copy.wait_send()

    for p in range(pieces):
        arrived(x_recv.at[p], xs_send.at[p])
        arrived(y_recv.at[p], ys_send.at[p])
        arrived(z_all.at[p, pl.ds(1, nz - 1)], zs_send.at[p])
        arrived(rel_own.at[p, x, pl.ds(0, NY - 1)], ya_send.at[p])
        arrived(rel_own.at[p, pl.ds(0, NX - 1)], xa_send.at[p])
        arrived(rel_own.at[p], ca_send.at[p])
    gs_copy.wait()
    gd_copy.wait()
    arrived(rel_own, out_sem.at[2])
    for p in range(pieces):
        arrived(rel_out.at[1 - core, p], ca_recv.at[p])


def store_kernel(
    rels, gs_in, gd_in, rel_in, gs_out, gd_out, rel_out, rel_b, rel_f, gs_v, gd_v, in_sem, out_sem
):
    loads = [
        pltpu.make_async_copy(rel_in, rel_b, in_sem.at[0]),
        pltpu.make_async_copy(gs_in, gs_v, in_sem.at[1]),
        pltpu.make_async_copy(gd_in, gd_v, in_sem.at[2]),
    ]
    stores = [
        pltpu.make_async_copy(rel_f, rel_out, out_sem.at[0]),
        pltpu.make_async_copy(gs_v, gs_out, out_sem.at[1]),
        pltpu.make_async_copy(gd_v, gd_out, out_sem.at[2]),
    ]
    for load in loads:
        load.start()
    half = rel_b.shape[2]
    loads[0].wait()
    for h in range(2):
        rel_f[:, h * half:(h + 1) * half] = rel_b[h, 0:rels, :].astype(F32)
    stores[0].start()
    for k in (1, 2):
        loads[k].wait()
        stores[k].start()
    for store in stores:
        store.wait()


def body(src_embed, dst_embed, relation, src_index, dst_index, rel_index, neg_index, edge_count):
    ent, width = src_embed.shape
    rels = relation.shape[0]
    steps = src_index.shape[2]
    nz = lax.axis_size("grp") // NX * ZLO
    half = width // 2
    pieces = -(-rels // (NX * NY * CHUNK))
    rows_mm = -(-rels // 128) * 128
    xrows = NY * CHUNK
    prows = NX * xrows
    tables = [t.reshape(steps, ent) for t in (src_index, dst_index, rel_index, neg_index)]
    vmem = pltpu.VMEM
    dma = pltpu.SemaphoreType.DMA
    block = vmem((ent, width), BF16)
    scratch = [
        vmem((4, ent, width), BF16),
        block,
        block,
        vmem((rels, width), F32),
        vmem((rows_mm, width), F32),
        vmem((2 * width, rows_mm), BF16),
        vmem((width, ent), BF16),
        vmem((4, steps, ent), jnp.int32),
        vmem((4, steps, ent), jnp.int32),
        vmem((1, steps), jnp.int32),
        vmem((1, steps), jnp.int32),
        vmem((ent, 4 * ent), BF16),
        vmem((rows_mm, 4 * ent), BF16),
        vmem((4, width, ent), BF16),
        vmem((4, width, ent), F32),
        vmem((4, width, ent), BF16),
        vmem((4, ent, 1), F32),
        vmem((4, ent, ent), BF16),
        vmem((width, 4 * ent), BF16),
        vmem((width, 4 * ent), BF16),
        vmem((4, ent, width), F32),
        vmem((ent, width), F32),
        vmem((2, pieces * prows, half), F32),
        block, block, block, block, block, block, block, block,
        vmem((pieces, prows, half), F32),
        vmem((pieces, prows, half), BF16),
        vmem((pieces, NX - 1, xrows, half), BF16),
        vmem((pieces, xrows, half), BF16),
        vmem((pieces, NY - 1, CHUNK, half), BF16),
        vmem((pieces, nz, CHUNK, half), F32),
        vmem((pieces, NX, NY, CHUNK, half), BF16),
        dma((5,)),
        dma((3,)),
        dma((3, 2)),
        dma((4, 2)),
        dma((3,)), dma((3,)),
        dma((4,)), dma((4,)),
    ] + [dma((pieces,))] * 14
    anywhere = pl.BlockSpec(memory_space=pl.ANY)
    grad = jax.ShapeDtypeStruct((ent, width), F32)
    grad_src, grad_dst, rel_parts = pl.pallas_call(
        functools.partial(kernel, nz, rels, rows_mm, pieces),
        out_shape=(
            grad, grad, jax.ShapeDtypeStruct((2, pieces, NX, NY, CHUNK, half), BF16)
        ),
        in_specs=[anywhere] * 8,
        out_specs=(anywhere,) * 3,
        scratch_shapes=scratch,
        compiler_params=pltpu.CompilerParams(
            collective_id=0, has_side_effects=True, vmem_limit_bytes=56 * 1024 * 1024
        ),
    )(src_embed, dst_embed, relation, *tables, edge_count.reshape(1, steps))
    rel_parts = rel_parts.reshape(2, pieces * prows, half)
    return pl.pallas_call(
        functools.partial(store_kernel, rels),
        out_shape=(grad, grad, jax.ShapeDtypeStruct((rels, width), F32)),
        in_specs=[anywhere] * 3,
        out_specs=(anywhere,) * 3,
        scratch_shapes=[
            vmem(rel_parts.shape, BF16), vmem((rels, width), F32),
            vmem((ent, width), F32), vmem((ent, width), F32), dma((3,)), dma((3,)),
        ],
        compiler_params=pltpu.CompilerParams(vmem_limit_bytes=56 * 1024 * 1024),
    )(grad_src, grad_dst, rel_parts)


def solution(mesh):
    in_specs = (
        P(("grp", "blk"), None),
        P(("grp", "blk"), None),
        P(),
        P("grp", "blk", None, None),
        P("grp", "blk", None, None),
        P("grp", "blk", None, None),
        P("grp", "blk", None, None),
        P("grp", "blk", None),
    )
    out_specs = (P(("grp", "blk"), None), P(("grp", "blk"), None), P())
    return jax.shard_map(body, mesh=mesh, in_specs=in_specs, out_specs=out_specs, check_vma=False)
```

```python
import functools

import jax
import jax.numpy as jnp
from jax import lax
from jax.experimental import pallas as pl
from jax.experimental.pallas import tpu as pltpu
from jax.sharding import PartitionSpec as P

MESH = pl.DeviceIdType.MESH
F32 = jnp.float32
BF16 = jnp.bfloat16
NX = 4
NY = 8
ZLO = 2
CHUNK = 16
STEP = 128


def nt(a, b):
    return lax.dot_general(a, b, (((1,), (1,)), ((), ())), preferred_element_type=F32)


def nn(a, b):
    return jnp.dot(a, b, preferred_element_type=F32)


def kernel(
    nz, rels, rows_mm, pieces,
    src_hbm, dst_hbm, rel_hbm, si_hbm, di_hbm, ri_hbm, ni_hbm, ec_hbm,
    gs_out, gd_out, rel_out,
    part, src_v, src_far, rel_v, rel_pad, rel_t, src_t, idx, idx_far, ec, ec_far,
    ohs, ohr, sr, rr, qt, weight, pulls, back_v, value, gw, gs, gr,
    gs_send, gs_recv, ga_send, ga_recv, gb_send, gb_recv, gh_send, gh_recv,
    half_recv, xs, x_recv, ys, y_recv, z_all, rel_own,
    in_sem, out_sem, part_send, part_recv, far_send, far_recv,
    g_send, g_recv, h_send, h_recv, h_out, s_send, s_recv,
    xs_send, xs_recv, ys_send, ys_recv, zs_send, zs_recv,
    ya_send, ya_recv, xa_send, xa_recv, ca_send, ca_recv,
):
    ent, width = dst_hbm.shape
    half = width // 2
    yrows = CHUNK
    xrows = NY * yrows
    prows = NX * xrows
    nchip = ZLO * NY
    grp, blk = lax.axis_index("grp"), lax.axis_index("blk")
    core = lax.rem(blk, 2)
    chip = blk // 2
    y = lax.rem(chip, NY)
    z = (grp // NX) * ZLO + chip // NY
    x = lax.rem(grp, NX)
    even = core == 0
    nxt = lax.rem(chip + 1, nchip) * 2 + core
    prv = lax.rem(chip + nchip - 1, nchip) * 2 + core
    sib = (grp, chip * 2 + 1 - core)

    def at_x(i):
        return ((grp // NX) * NX + i, blk)

    def at_y(i):
        return (grp, (chip // NY) * NY * 2 + i * 2 + core)

    def at_z(i):
        return ((i // ZLO) * NX + x, lax.rem(i, ZLO) * NY * 2 + y * 2 + core)

    def ring(place, size):
        steps = sorted(range(1, size), key=lambda k: -min(k, size - k))
        return [(k, lax.rem(place + k, size)) for k in steps]

    x_others, y_others, z_others = ring(x, NX), ring(y, NY), ring(z, nz)

    def remote(source, target, send, recv, device):
        return pltpu.make_async_remote_copy(
            src_ref=source, dst_ref=target, send_sem=send, recv_sem=recv,
            device_id=device, device_id_type=MESH,
        )

    def arrived(buffer, recv):
        pltpu.make_async_copy(buffer, buffer, recv).wait()

    own = [(si_hbm, 0), (di_hbm, 1), (ri_hbm, 2), (ni_hbm, 3)]
    loads = [
        pltpu.make_async_copy(ec_hbm, ec, in_sem.at[3]),
        pltpu.make_async_copy(dst_hbm, part.at[0], in_sem.at[2]),
        pltpu.make_async_copy(src_hbm, src_v, in_sem.at[1]),
        pltpu.make_async_copy(rel_hbm, rel_v, in_sem.at[0]),
    ]
    tables_in = [pltpu.make_async_copy(ref, idx.at[k], in_sem.at[4]) for ref, k in own]
    for load in loads[:2] + tables_in + loads[2:]:
        load.start()
    barrier = pltpu.get_barrier_semaphore()
    greet = [sib, (grp, nxt), (grp, prv)]
    greet += [at_x(i) for _, i in x_others] + [at_y(i) for _, i in y_others]
    greet += [at_z(i) for _, i in z_others]
    for device in greet:
        pl.semaphore_signal(barrier, inc=1, device_id=device, device_id_type=MESH)
    if rows_mm < pieces * prows:
        gr[:, rows_mm:, :] = jnp.zeros((2, pieces * prows - rows_mm, half), F32)
    tail = rels // 8 * 8
    rel_pad[tail:, :] = jnp.zeros((rows_mm - tail, width), F32)

    def tile_of(w):
        if w in (0, 3):
            return w
        return jnp.where(even, 3 - w, w)

    def row_of(k, w):
        row = idx[k, pl.ds(tile_of(w), 1), :]
        if w == 3:
            row = jnp.where(even, idx_far[k, 3:4, :], row)
        return row

    def live_of(w):
        counts = ec[...].astype(F32)
        if w == 3:
            counts = jnp.where(even, ec_far[...].astype(F32), counts)
        place = lax.broadcasted_iota(jnp.int32, counts.shape, 1)
        count = jnp.sum(jnp.where(place == tile_of(w), counts, 0.0), axis=1, keepdims=True)
        slot = lax.broadcasted_iota(jnp.int32, (1, ent), 1).astype(F32)
        return slot < count

    def lanes(w):
        return pl.ds(w * ent, ent)

    def tables(w):
        rows = lax.broadcasted_iota(jnp.int32, (ent, ent), 0)
        ohs[:, lanes(w)] = (rows == jnp.where(live_of(w), row_of(0, w), -1)).astype(BF16)
        chosen = (rows == row_of(3, w)).astype(F32)
        weight[w] = jnp.sum(chosen, axis=1, keepdims=True) * (1.0 / ent)
        rows = lax.broadcasted_iota(jnp.int32, (rows_mm, ent), 0)
        ohr[:, lanes(w)] = (rows == row_of(2, w)).astype(BF16)

    def gather(w):
        picked = nn(src_t[...], ohs[:, lanes(w)])
        both = nn(rel_t[...], ohr[:, lanes(w)])
        scale = both[0:width] + both[width:]
        sr[w] = picked.astype(BF16)
        rr[w] = scale
        qt[w] = (picked * scale).astype(BF16)

    def score(w, slot, h):
        mid = ent // 2
        for low in range(h * mid, (h + 1) * mid, min(STEP, mid)):
            size = min(STEP, mid)
            scores = nn(part[slot, low:low + size, :], qt[w])
            rows = low + lax.broadcasted_iota(jnp.int32, (size, ent), 0)
            decay = jnp.exp(jnp.minimum(-scores, 87.0))
            share = weight[w, low:low + size]
            share = jnp.where(rows == row_of(1, w), share - decay, share)
            inverse = pl.reciprocal(1.0 + decay, approx=True)
            pulls[w, low:low + size] = (inverse * share).astype(BF16)

    def pull_half(w, slot, h):
        return nn(part[slot, halves[h], :].T, pulls[w, halves[h], :])

    def give(w, dquery):
        back_v[:, lanes(w)] = (dquery * rr[w]).astype(BF16)
        value[:, lanes(w)] = (dquery * sr[w].astype(F32)).astype(BF16)

    def finish(w, slot):
        score(w, slot, 0)
        score(w, slot, 1)
        give(w, nn(part[slot].T, pulls[w]))

    def grow(p, first, last):
        low, high = p * prows, min((p + 1) * prows, rows_mm)
        span = pl.ds(first * ent, (last - first) * ent)
        grown = nt(ohr[low:high, span], value[:, span])
        for h in range(2):
            grown_half = grown[:, h * half:(h + 1) * half]
            if first == 0:
                gr[h, low:high, :] = grown_half
            else:
                gr[h, low:high, :] += grown_half

    swaps = [
        remote(
            gr.at[1 - core, pl.ds(p * prows, prows)], half_recv.at[p],
            s_send.at[p], s_recv.at[p], sib,
        )
        for p in range(pieces)
    ]

    arrived(idx, in_sem.at[4])
    loads[0].wait()
    for w in range(3):
        tables(w)

    pl.semaphore_wait(barrier, len(greet))

    direct = 2 - core
    other = 1 + core
    halves = [pl.ds(0, ent // 2), pl.ds(ent // 2, ent // 2)]

    def send_part(source, slot, h, send, device):
        return remote(
            source.at[halves[h]], part.at[slot, halves[h]], part_send.at[send, h],
            part_recv.at[slot, h], device,
        )

    def arrived_part(slot, h):
        arrived(part.at[slot, halves[h]], part_recv.at[slot, h])

    send_next = [send_part(part.at[0], direct, h, 0, (grp, nxt)) for h in range(2)]
    send_sib = [send_part(part.at[0], 3, h, 1, sib) for h in range(2)]
    forward = [send_part(part.at[direct], direct, h, 2, sib) for h in range(2)]
    loads[1].wait()
    for copy in send_next:
        copy.start()
    far = [remote(src_hbm, src_far, far_send.at[0], far_recv.at[0], (grp, prv))]
    far += [remote(ec_hbm, ec_far, far_send.at[1], far_recv.at[1], (grp, prv))]
    far += [
        remote(ref, idx_far.at[k], far_send.at[2], far_recv.at[2], (grp, prv))
        for ref, k in own
    ]

    @pl.when(even)
    def _():
        for copy in send_sib + far:
            copy.start()

    for load in loads[2:]:
        load.wait()
    rel_pad[0:rels, :] = rel_v[...]
    turned = rel_pad[...].T
    high = turned.astype(BF16)
    rel_t[0:width, :] = high
    rel_t[width:, :] = (turned - high.astype(F32)).astype(BF16)
    src_t[...] = src_v[...].T

    gather(0)
    finish(0, 0)
    for p in range(pieces):
        grow(p, 0, 1)
    gather(1)
    gather(2)

    @pl.when(even)
    def _():
        arrived(idx_far, far_recv.at[2])
        arrived(ec_far, far_recv.at[1])
        arrived(src_far, far_recv.at[0])
        src_t[...] = src_far[...].T

    tables(3)
    gather(3)

    for h in range(2):
        arrived_part(direct, h)
        forward[h].start()

    @pl.when(core == 1)
    def _():
        arrived_part(3, 0)
        arrived_part(3, 1)

    finish(1, 2 + core)
    for p in range(pieces):
        grow(p, 1, 2)
    arrived_part(other, 0)
    score(2, 1, 0)
    score(3, other, 0)
    first = [pull_half(2, 1, 0), pull_half(3, other, 0)]
    arrived_part(other, 1)
    score(2, 1, 1)
    score(3, other, 1)
    give(2, first[0] + pull_half(2, 1, 1))
    give(3, first[1] + pull_half(3, other, 1))
    for p in range(pieces):
        grow(p, 2, 4)
        swaps[p].start()

    sent = send_next + forward + swaps

    def rows_at(i, size):
        return pl.ds(pl.multiple_of(i * size, size), size)

    for w in (2, 3):
        gw[w] = nt(pulls[w], qt[w])
    ga_send[...] = (gw[3] + jnp.where(even, gw[2], 0.0)).astype(BF16)
    pair_copy = remote(ga_send, ga_recv, g_send.at[1], g_recv.at[1], sib)
    pair_copy.start()
    last = nt(ohs[:, lanes(3)], back_v[:, lanes(3)])
    gs_send[...] = last.astype(BF16)
    src_copy = remote(gs_send, gs_recv, g_send.at[2], g_recv.at[2], (grp, nxt))

    @pl.when(even)
    def _():
        src_copy.start()

    gw[1] = nt(pulls[1], qt[1])
    gb_send[...] = gw[1].astype(BF16)
    home_copy = remote(gb_send, gb_recv, g_send.at[0], g_recv.at[0], sib)

    @pl.when(core == 1)
    def _():
        home_copy.start()

    for p in range(pieces):
        arrived(half_recv.at[p], s_recv.at[p])
        xs[p] = (gr[core, p * prows:(p + 1) * prows, :] + half_recv[p]).astype(BF16)
        for k, i in x_others:
            remote(
                xs.at[p, rows_at(i, xrows)], x_recv.at[p, k - 1], xs_send.at[p], xs_recv.at[p], at_x(i)
            ).start()

    arrived(ga_recv, g_recv.at[1])
    gh_send[...] = (gw[1 + core] + ga_recv[...].astype(F32)).astype(BF16)
    sent.append(pair_copy)
    gw[0] = nt(pulls[0], qt[0])
    own_slots = pl.ds(0, 3 * ent)
    gs[...] = nt(ohs[:, own_slots], back_v[:, own_slots])

    @pl.when(core == 1)
    def _():
        gs[...] += last

    for p in range(pieces):
        total = xs[p, rows_at(x, xrows), :].astype(F32)
        arrived(x_recv.at[p], xs_recv.at[p])
        for k in range(NX - 1):
            total = total + x_recv[p, k].astype(F32)
        ys[p] = total.astype(BF16)
        for k, i in y_others:
            remote(
                ys.at[p, rows_at(i, yrows)], y_recv.at[p, k - 1], ys_send.at[p], ys_recv.at[p], at_y(i)
            ).start()

    for p in range(pieces):
        total = ys[p, rows_at(y, yrows), :].astype(F32)
        arrived(y_recv.at[p], ys_recv.at[p])
        for k in range(NY - 1):
            total = total + y_recv[p, k].astype(F32)
        z_all[p, 0] = total
        for k, i in z_others:
            remote(
                z_all.at[p, 0], z_all.at[p, k], zs_send.at[p], zs_recv.at[p], at_z(i)
            ).start()

    @pl.when(even)
    def _():
        arrived(gs_recv, g_recv.at[2])
        gs[...] += gs_recv[...].astype(F32)
        arrived(gb_recv, g_recv.at[0])
        gw[0] = gw[0] + gb_recv[...].astype(F32)

    gs_copy = pltpu.make_async_copy(gs, gs_out, out_sem.at[0])
    gs_copy.start()
    for p in range(pieces):
        arrived(z_all.at[p, pl.ds(1, nz - 1)], zs_recv.at[p])
        total = z_all[p, z]
        for i in range(1, nz):
            total = total + z_all[p, lax.rem(z + nz - i, nz)]
        piece = rel_own.at[p, x, y]
        piece[...] = total.astype(BF16)
        for _, i in y_others:
            remote(piece, piece, ya_send.at[p], ya_recv.at[p], at_y(i)).start()

    for p in range(pieces):
        arrived(rel_own.at[p, x, pl.ds(0, NY - 1)], ya_recv.at[p])
        piece = rel_own.at[p, x]
        for _, i in x_others:
            remote(piece, piece, xa_send.at[p], xa_recv.at[p], at_x(i)).start()
    homeward = [
        remote(gh_send.at[part_rows], gh_recv.at[part_rows], h_send.at[h], h_recv.at[h], (grp, prv))
        for h, part_rows in enumerate(halves)
    ]
    for copy in homeward:
        copy.start()
    sent += homeward
    for p in range(pieces):
        arrived(rel_own.at[p, pl.ds(0, NX - 1)], xa_recv.at[p])
        remote(rel_own.at[p], rel_out.at[core, p], ca_send.at[p], ca_recv.at[p], sib).start()
        pltpu.make_async_copy(rel_own.at[p], rel_out.at[core, p], out_sem.at[2]).start()

    gd_copies = []
    for h, part_rows in enumerate(halves):
        arrived(gh_recv.at[part_rows], h_recv.at[h])
        gw[0, part_rows, :] = gw[0, part_rows, :] + gh_recv[part_rows, :].astype(F32)
        gd_copies.append(
            pltpu.make_async_copy(gw.at[0, part_rows], gd_out.at[part_rows], h_out.at[h])
        )
        gd_copies[h].start()

    for copy in sent:
        copy.wait_send()

    @pl.when(even)
    def _():
        for copy in send_sib + far[:2]:
            copy.wait_send()
        arrived(idx, far_send.at[2])
        src_copy.wait_send()

    @pl.when(core == 1)
    def _():
        home_copy.wait_send()

    for p in range(pieces):
        arrived(x_recv.at[p], xs_send.at[p])
        arrived(y_recv.at[p], ys_send.at[p])
        arrived(z_all.at[p, pl.ds(1, nz - 1)], zs_send.at[p])
        arrived(rel_own.at[p, x, pl.ds(0, NY - 1)], ya_send.at[p])
        arrived(rel_own.at[p, pl.ds(0, NX - 1)], xa_send.at[p])
        arrived(rel_own.at[p], ca_send.at[p])
    gs_copy.wait()
    for copy in gd_copies:
        copy.wait()
    arrived(rel_own, out_sem.at[2])
    for p in range(pieces):
        arrived(rel_out.at[1 - core, p], ca_recv.at[p])


def store_kernel(
    rels, gs_in, gd_in, rel_in, gs_out, gd_out, rel_out, rel_b, rel_f, gs_v, gd_v, in_sem, out_sem
):
    pieces, rows, half = rel_b.shape[1:]
    spans = [(p * rows, min((p + 1) * rows, rels)) for p in range(pieces)]
    loads = [
        pltpu.make_async_copy(rel_in.at[h, p], rel_b.at[h, p], in_sem.at[2 + 2 * p + h])
        for p in range(pieces) for h in range(2)
    ] + [
        pltpu.make_async_copy(gs_in, gs_v, in_sem.at[0]),
        pltpu.make_async_copy(gd_in, gd_v, in_sem.at[1]),
    ]
    for load in loads:
        load.start()
    stores = []

    def store(source, target):
        stores.append(pltpu.make_async_copy(source, target, out_sem.at[len(stores)]))
        stores[-1].start()

    for p, (low, high) in enumerate(spans):
        for h in range(2):
            loads[2 * p + h].wait()
            rel_f[low:high, h * half:(h + 1) * half] = rel_b[h, p, 0:high - low, :].astype(F32)
        store(rel_f.at[low:high], rel_out.at[low:high])
    for load, source, target in ((loads[-2], gs_v, gs_out), (loads[-1], gd_v, gd_out)):
        load.wait()
        store(source, target)
    for copy in stores:
        copy.wait()


def body(src_embed, dst_embed, relation, src_index, dst_index, rel_index, neg_index, edge_count):
    ent, width = src_embed.shape
    rels = relation.shape[0]
    steps = src_index.shape[2]
    nz = lax.axis_size("grp") // NX * ZLO
    half = width // 2
    pieces = -(-rels // (NX * NY * CHUNK))
    rows_mm = -(-rels // 128) * 128
    xrows = NY * CHUNK
    prows = NX * xrows
    tables = [t.reshape(steps, ent) for t in (src_index, dst_index, rel_index, neg_index)]
    vmem = pltpu.VMEM
    dma = pltpu.SemaphoreType.DMA
    block = vmem((ent, width), BF16)
    scratch = [
        vmem((4, ent, width), BF16),
        block,
        block,
        vmem((rels, width), F32),
        vmem((rows_mm, width), F32),
        vmem((2 * width, rows_mm), BF16),
        vmem((width, ent), BF16),
        vmem((4, steps, ent), jnp.int32),
        vmem((4, steps, ent), jnp.int32),
        vmem((1, steps), jnp.int32),
        vmem((1, steps), jnp.int32),
        vmem((ent, 4 * ent), BF16),
        vmem((rows_mm, 4 * ent), BF16),
        vmem((4, width, ent), BF16),
        vmem((4, width, ent), F32),
        vmem((4, width, ent), BF16),
        vmem((4, ent, 1), F32),
        vmem((4, ent, ent), BF16),
        vmem((width, 4 * ent), BF16),
        vmem((width, 4 * ent), BF16),
        vmem((4, ent, width), F32),
        vmem((ent, width), F32),
        vmem((2, pieces * prows, half), F32),
        block, block, block, block, block, block, block, block,
        vmem((pieces, prows, half), F32),
        vmem((pieces, prows, half), BF16),
        vmem((pieces, NX - 1, xrows, half), BF16),
        vmem((pieces, xrows, half), BF16),
        vmem((pieces, NY - 1, CHUNK, half), BF16),
        vmem((pieces, nz, CHUNK, half), F32),
        vmem((pieces, NX, NY, CHUNK, half), BF16),
        dma((5,)),
        dma((3,)),
        dma((3, 2)),
        dma((4, 2)),
        dma((3,)), dma((3,)),
        dma((3,)), dma((3,)),
        dma((2,)), dma((2,)), dma((2,)),
    ] + [dma((pieces,))] * 14
    anywhere = pl.BlockSpec(memory_space=pl.ANY)
    grad = jax.ShapeDtypeStruct((ent, width), F32)
    grad_src, grad_dst, rel_parts = pl.pallas_call(
        functools.partial(kernel, nz, rels, rows_mm, pieces),
        out_shape=(
            grad, grad, jax.ShapeDtypeStruct((2, pieces, NX, NY, CHUNK, half), BF16)
        ),
        in_specs=[anywhere] * 8,
        out_specs=(anywhere,) * 3,
        scratch_shapes=scratch,
        compiler_params=pltpu.CompilerParams(
            collective_id=0, has_side_effects=True, vmem_limit_bytes=56 * 1024 * 1024
        ),
    )(src_embed, dst_embed, relation, *tables, edge_count.reshape(1, steps))
    rel_parts = rel_parts.reshape(2, pieces, prows, half)
    return pl.pallas_call(
        functools.partial(store_kernel, rels),
        out_shape=(grad, grad, jax.ShapeDtypeStruct((rels, width), F32)),
        in_specs=[anywhere] * 3,
        out_specs=(anywhere,) * 3,
        scratch_shapes=[
            vmem(rel_parts.shape, BF16), vmem((rels, width), F32),
            vmem((ent, width), F32), vmem((ent, width), F32),
            dma((2 + 2 * pieces,)), dma((2 + pieces,)),
        ],
        compiler_params=pltpu.CompilerParams(vmem_limit_bytes=56 * 1024 * 1024),
    )(grad_src, grad_dst, rel_parts)


def solution(mesh):
    in_specs = (
        P(("grp", "blk"), None),
        P(("grp", "blk"), None),
        P(),
        P("grp", "blk", None, None),
        P("grp", "blk", None, None),
        P("grp", "blk", None, None),
        P("grp", "blk", None, None),
        P("grp", "blk", None),
    )
    out_specs = (P(("grp", "blk"), None), P(("grp", "blk"), None), P())
    return jax.shard_map(body, mesh=mesh, in_specs=in_specs, out_specs=out_specs, check_vma=False)
```

```python
import functools

import jax
import jax.numpy as jnp
from jax import lax
from jax.experimental import pallas as pl
from jax.experimental.pallas import tpu as pltpu
from jax.sharding import PartitionSpec as P

MESH = pl.DeviceIdType.MESH
F32 = jnp.float32
BF16 = jnp.bfloat16
NX = 4
NY = 8
ZLO = 2
CHUNK = 16
STEP = 128


def nt(a, b):
    return lax.dot_general(a, b, (((1,), (1,)), ((), ())), preferred_element_type=F32)


def nn(a, b):
    return jnp.dot(a, b, preferred_element_type=F32)


def kernel(
    nz, rels, rows_mm, pieces,
    src_hbm, dst_hbm, rel_hbm, si_hbm, di_hbm, ri_hbm, ni_hbm, ec_hbm,
    gs_out, gd_out, rel_out,
    part, src_v, src_far, rel_v, rel_pad, rel_t, src_t, idx, idx_far, ec, ec_far,
    ohs, ohr, sr, rr, qt, weight, pulls, back_v, value, gw, gs, gr,
    gs_send, gs_recv, ga_send, ga_recv, gb_send, gb_recv, gh_send, gh_recv,
    half_recv, xs, x_recv, ys, y_recv, z_all, rel_own,
    in_sem, out_sem, part_send, part_recv, far_send, far_recv,
    g_send, g_recv, h_send, h_recv, h_out, s_send, s_recv,
    xs_send, xs_recv, ys_send, ys_recv, zs_send, zs_recv,
    ya_send, ya_recv, xa_send, xa_recv, ca_send, ca_recv,
):
    ent, width = dst_hbm.shape
    half = width // 2
    yrows = CHUNK
    xrows = NY * yrows
    prows = NX * xrows
    nchip = ZLO * NY
    grp, blk = lax.axis_index("grp"), lax.axis_index("blk")
    core = lax.rem(blk, 2)
    chip = blk // 2
    y = lax.rem(chip, NY)
    z = (grp // NX) * ZLO + chip // NY
    x = lax.rem(grp, NX)
    even = core == 0
    nxt = lax.rem(chip + 1, nchip) * 2 + core
    prv = lax.rem(chip + nchip - 1, nchip) * 2 + core
    sib = (grp, chip * 2 + 1 - core)

    def at_x(i):
        return ((grp // NX) * NX + i, blk)

    def at_y(i):
        return (grp, (chip // NY) * NY * 2 + i * 2 + core)

    def at_z(i):
        return ((i // ZLO) * NX + x, lax.rem(i, ZLO) * NY * 2 + y * 2 + core)

    def ring(place, size):
        steps = sorted(range(1, size), key=lambda k: -min(k, size - k))
        return [(k, lax.rem(place + k, size)) for k in steps]

    x_others, y_others, z_others = ring(x, NX), ring(y, NY), ring(z, nz)

    def remote(source, target, send, recv, device):
        return pltpu.make_async_remote_copy(
            src_ref=source, dst_ref=target, send_sem=send, recv_sem=recv,
            device_id=device, device_id_type=MESH,
        )

    def arrived(buffer, recv):
        pltpu.make_async_copy(buffer, buffer, recv).wait()

    own = [(si_hbm, 0), (di_hbm, 1), (ri_hbm, 2), (ni_hbm, 3)]
    loads = [
        pltpu.make_async_copy(ec_hbm, ec, in_sem.at[3]),
        pltpu.make_async_copy(dst_hbm, part.at[0], in_sem.at[2]),
        pltpu.make_async_copy(src_hbm, src_v, in_sem.at[1]),
        pltpu.make_async_copy(rel_hbm, rel_v, in_sem.at[0]),
    ]
    tables_in = [pltpu.make_async_copy(ref, idx.at[k], in_sem.at[4]) for ref, k in own]
    for load in loads[:2] + tables_in + loads[2:]:
        load.start()
    barrier = pltpu.get_barrier_semaphore()
    greet = [sib, (grp, nxt), (grp, prv)]
    greet += [at_x(i) for _, i in x_others] + [at_y(i) for _, i in y_others]
    greet += [at_z(i) for _, i in z_others]
    for device in greet:
        pl.semaphore_signal(barrier, inc=1, device_id=device, device_id_type=MESH)
    if rows_mm < pieces * prows:
        gr[:, rows_mm:, :] = jnp.zeros((2, pieces * prows - rows_mm, half), F32)
    tail = rels // 8 * 8
    rel_pad[tail:, :] = jnp.zeros((rows_mm - tail, width), F32)

    def tile_of(w):
        if w in (0, 3):
            return w
        return jnp.where(even, 3 - w, w)

    def row_of(k, w):
        row = idx[k, pl.ds(tile_of(w), 1), :]
        if w == 3:
            row = jnp.where(even, idx_far[k, 3:4, :], row)
        return row

    def live_of(w):
        counts = ec[...].astype(F32)
        if w == 3:
            counts = jnp.where(even, ec_far[...].astype(F32), counts)
        place = lax.broadcasted_iota(jnp.int32, counts.shape, 1)
        count = jnp.sum(jnp.where(place == tile_of(w), counts, 0.0), axis=1, keepdims=True)
        slot = lax.broadcasted_iota(jnp.int32, (1, ent), 1).astype(F32)
        return slot < count

    def lanes(w):
        return pl.ds(w * ent, ent)

    def tables(w):
        rows = lax.broadcasted_iota(jnp.int32, (ent, ent), 0)
        ohs[:, lanes(w)] = (rows == jnp.where(live_of(w), row_of(0, w), -1)).astype(BF16)
        chosen = (rows == row_of(3, w)).astype(F32)
        weight[w] = jnp.sum(chosen, axis=1, keepdims=True) * (1.0 / ent)
        rows = lax.broadcasted_iota(jnp.int32, (rows_mm, ent), 0)
        ohr[:, lanes(w)] = (rows == row_of(2, w)).astype(BF16)

    def gather(w):
        picked = nn(src_t[...], ohs[:, lanes(w)])
        both = nn(rel_t[...], ohr[:, lanes(w)])
        scale = both[0:width] + both[width:]
        sr[w] = picked.astype(BF16)
        rr[w] = scale
        qt[w] = (picked * scale).astype(BF16)

    def score(w, slot, h):
        mid = ent // 2
        for low in range(h * mid, (h + 1) * mid, min(STEP, mid)):
            size = min(STEP, mid)
            scores = nn(part[slot, low:low + size, :], qt[w])
            rows = low + lax.broadcasted_iota(jnp.int32, (size, ent), 0)
            decay = jnp.exp(jnp.minimum(-scores, 87.0))
            share = weight[w, low:low + size]
            share = jnp.where(rows == row_of(1, w), share - decay, share)
            inverse = pl.reciprocal(1.0 + decay, approx=True)
            pulls[w, low:low + size] = (inverse * share).astype(BF16)

    def pull_half(w, slot, h):
        return nn(part[slot, halves[h], :].T, pulls[w, halves[h], :])

    def give(w, dquery):
        back_v[:, lanes(w)] = (dquery * rr[w]).astype(BF16)
        value[:, lanes(w)] = (dquery * sr[w].astype(F32)).astype(BF16)

    def finish(w, slot):
        score(w, slot, 0)
        score(w, slot, 1)
        give(w, nn(part[slot].T, pulls[w]))

    def grow(p, first, last):
        low, high = p * prows, min((p + 1) * prows, rows_mm)
        span = pl.ds(first * ent, (last - first) * ent)
        grown = nt(ohr[low:high, span], value[:, span])
        for h in range(2):
            grown_half = grown[:, h * half:(h + 1) * half]
            if first == 0:
                gr[h, low:high, :] = grown_half
            else:
                gr[h, low:high, :] += grown_half

    swaps = [
        remote(
            gr.at[1 - core, pl.ds(p * prows, prows)], half_recv.at[p],
            s_send.at[p], s_recv.at[p], sib,
        )
        for p in range(pieces)
    ]

    arrived(idx, in_sem.at[4])
    loads[0].wait()
    for w in range(3):
        tables(w)

    pl.semaphore_wait(barrier, len(greet))

    direct = 2 - core
    other = 1 + core
    halves = [pl.ds(0, ent // 2), pl.ds(ent // 2, ent // 2)]

    def send_part(source, slot, h, send, device):
        return remote(
            source.at[halves[h]], part.at[slot, halves[h]], part_send.at[send, h],
            part_recv.at[slot, h], device,
        )

    def arrived_part(slot, h):
        arrived(part.at[slot, halves[h]], part_recv.at[slot, h])

    send_next = [send_part(part.at[0], direct, h, 0, (grp, nxt)) for h in range(2)]
    send_sib = [send_part(part.at[0], 3, h, 1, sib) for h in range(2)]
    forward = [send_part(part.at[direct], direct, h, 2, sib) for h in range(2)]
    loads[1].wait()
    for copy in send_next:
        copy.start()
    far = [remote(src_hbm, src_far, far_send.at[0], far_recv.at[0], (grp, prv))]
    far += [remote(ec_hbm, ec_far, far_send.at[1], far_recv.at[1], (grp, prv))]
    far += [
        remote(ref, idx_far.at[k], far_send.at[2], far_recv.at[2], (grp, prv))
        for ref, k in own
    ]

    @pl.when(even)
    def _():
        for copy in send_sib + far:
            copy.start()

    for load in loads[2:]:
        load.wait()
    rel_pad[0:rels, :] = rel_v[...]
    turned = rel_pad[...].T
    high = turned.astype(BF16)
    rel_t[0:width, :] = high
    rel_t[width:, :] = (turned - high.astype(F32)).astype(BF16)
    src_t[...] = src_v[...].T

    gather(0)
    finish(0, 0)
    for p in range(pieces):
        grow(p, 0, 1)
    gather(1)
    gather(2)

    @pl.when(even)
    def _():
        arrived(idx_far, far_recv.at[2])
        arrived(ec_far, far_recv.at[1])
        arrived(src_far, far_recv.at[0])
        src_t[...] = src_far[...].T

    tables(3)
    gather(3)

    for h in range(2):
        arrived_part(direct, h)
        forward[h].start()

    @pl.when(core == 1)
    def _():
        arrived_part(3, 0)
        arrived_part(3, 1)

    finish(1, 2 + core)
    for p in range(pieces):
        grow(p, 1, 2)
    arrived_part(other, 0)
    score(2, 1, 0)
    score(3, other, 0)
    first = [pull_half(2, 1, 0), pull_half(3, other, 0)]
    arrived_part(other, 1)
    score(2, 1, 1)
    score(3, other, 1)
    give(2, first[0] + pull_half(2, 1, 1))
    give(3, first[1] + pull_half(3, other, 1))
    for p in range(pieces):
        grow(p, 2, 4)
        swaps[p].start()

    sent = send_next + forward + swaps

    def rows_at(i, size):
        return pl.ds(pl.multiple_of(i * size, size), size)

    for p in range(pieces):
        arrived(half_recv.at[p], s_recv.at[p])
        xs[p] = (gr[core, p * prows:(p + 1) * prows, :] + half_recv[p]).astype(BF16)
        for k, i in x_others:
            remote(
                xs.at[p, rows_at(i, xrows)], x_recv.at[p, k - 1], xs_send.at[p], xs_recv.at[p], at_x(i)
            ).start()

    last = nt(ohs[:, lanes(3)], back_v[:, lanes(3)])
    gs_send[...] = last.astype(BF16)
    src_copy = remote(gs_send, gs_recv, g_send.at[2], g_recv.at[2], (grp, nxt))

    @pl.when(even)
    def _():
        src_copy.start()

    for w in range(4):
        gw[w] = nt(pulls[w], qt[w])
    ga_send[...] = (gw[3] + jnp.where(even, gw[2], 0.0)).astype(BF16)
    pair_copy = remote(ga_send, ga_recv, g_send.at[1], g_recv.at[1], sib)
    pair_copy.start()
    sent.append(pair_copy)
    gb_send[...] = gw[1].astype(BF16)
    home_copy = remote(gb_send, gb_recv, g_send.at[0], g_recv.at[0], sib)

    @pl.when(core == 1)
    def _():
        home_copy.start()

    own_slots = pl.ds(0, 3 * ent)
    gs[...] = nt(ohs[:, own_slots], back_v[:, own_slots])

    @pl.when(core == 1)
    def _():
        gs[...] += last

    for p in range(pieces):
        total = xs[p, rows_at(x, xrows), :].astype(F32)
        arrived(x_recv.at[p], xs_recv.at[p])
        for k in range(NX - 1):
            total = total + x_recv[p, k].astype(F32)
        ys[p] = total.astype(BF16)
        for k, i in y_others:
            remote(
                ys.at[p, rows_at(i, yrows)], y_recv.at[p, k - 1], ys_send.at[p], ys_recv.at[p], at_y(i)
            ).start()

    arrived(ga_recv, g_recv.at[1])
    gh_send[...] = (gw[1 + core] + ga_recv[...].astype(F32)).astype(BF16)

    for p in range(pieces):
        total = ys[p, rows_at(y, yrows), :].astype(F32)
        arrived(y_recv.at[p], ys_recv.at[p])
        for k in range(NY - 1):
            total = total + y_recv[p, k].astype(F32)
        z_all[p, 0] = total
        for k, i in z_others:
            remote(
                z_all.at[p, 0], z_all.at[p, k], zs_send.at[p], zs_recv.at[p], at_z(i)
            ).start()

    @pl.when(even)
    def _():
        arrived(gs_recv, g_recv.at[2])
        gs[...] += gs_recv[...].astype(F32)
        arrived(gb_recv, g_recv.at[0])
        gw[0] = gw[0] + gb_recv[...].astype(F32)

    gs_copy = pltpu.make_async_copy(gs, gs_out, out_sem.at[0])
    gs_copy.start()
    for p in range(pieces):
        arrived(z_all.at[p, pl.ds(1, nz - 1)], zs_recv.at[p])
        total = z_all[p, z]
        for i in range(1, nz):
            total = total + z_all[p, lax.rem(z + nz - i, nz)]
        piece = rel_own.at[p, x, y]
        piece[...] = total.astype(BF16)
        for _, i in y_others:
            remote(piece, piece, ya_send.at[p], ya_recv.at[p], at_y(i)).start()

    for p in range(pieces):
        arrived(rel_own.at[p, x, pl.ds(0, NY - 1)], ya_recv.at[p])
        piece = rel_own.at[p, x]
        for _, i in x_others:
            remote(piece, piece, xa_send.at[p], xa_recv.at[p], at_x(i)).start()
    homeward = [
        remote(gh_send.at[part_rows], gh_recv.at[part_rows], h_send.at[h], h_recv.at[h], (grp, prv))
        for h, part_rows in enumerate(halves)
    ]
    for copy in homeward:
        copy.start()
    sent += homeward
    for p in range(pieces):
        arrived(rel_own.at[p, pl.ds(0, NX - 1)], xa_recv.at[p])
        remote(rel_own.at[p], rel_out.at[core, p], ca_send.at[p], ca_recv.at[p], sib).start()
        pltpu.make_async_copy(rel_own.at[p], rel_out.at[core, p], out_sem.at[2]).start()

    gd_copies = []
    for h, part_rows in enumerate(halves):
        arrived(gh_recv.at[part_rows], h_recv.at[h])
        gw[0, part_rows, :] = gw[0, part_rows, :] + gh_recv[part_rows, :].astype(F32)
        gd_copies.append(
            pltpu.make_async_copy(gw.at[0, part_rows], gd_out.at[part_rows], h_out.at[h])
        )
        gd_copies[h].start()

    for copy in sent:
        copy.wait_send()

    @pl.when(even)
    def _():
        for copy in send_sib + far[:2]:
            copy.wait_send()
        arrived(idx, far_send.at[2])
        src_copy.wait_send()

    @pl.when(core == 1)
    def _():
        home_copy.wait_send()

    for p in range(pieces):
        arrived(x_recv.at[p], xs_send.at[p])
        arrived(y_recv.at[p], ys_send.at[p])
        arrived(z_all.at[p, pl.ds(1, nz - 1)], zs_send.at[p])
        arrived(rel_own.at[p, x, pl.ds(0, NY - 1)], ya_send.at[p])
        arrived(rel_own.at[p, pl.ds(0, NX - 1)], xa_send.at[p])
        arrived(rel_own.at[p], ca_send.at[p])
    gs_copy.wait()
    for copy in gd_copies:
        copy.wait()
    arrived(rel_own, out_sem.at[2])
    for p in range(pieces):
        arrived(rel_out.at[1 - core, p], ca_recv.at[p])


def store_kernel(
    rels, gs_in, gd_in, rel_in, gs_out, gd_out, rel_out, rel_b, rel_f, gs_v, gd_v, in_sem, out_sem
):
    pieces, rows, half = rel_b.shape[1:]
    spans = [(p * rows, min((p + 1) * rows, rels)) for p in range(pieces)]
    loads = [
        pltpu.make_async_copy(rel_in.at[h, p], rel_b.at[h, p], in_sem.at[2 + 2 * p + h])
        for p in range(pieces) for h in range(2)
    ] + [
        pltpu.make_async_copy(gs_in, gs_v, in_sem.at[0]),
        pltpu.make_async_copy(gd_in, gd_v, in_sem.at[1]),
    ]
    for load in loads:
        load.start()
    stores = []

    def store(source, target):
        stores.append(pltpu.make_async_copy(source, target, out_sem.at[len(stores)]))
        stores[-1].start()

    for p, (low, high) in enumerate(spans):
        for h in range(2):
            loads[2 * p + h].wait()
            rel_f[low:high, h * half:(h + 1) * half] = rel_b[h, p, 0:high - low, :].astype(F32)
        store(rel_f.at[low:high], rel_out.at[low:high])
    for load, source, target in ((loads[-2], gs_v, gs_out), (loads[-1], gd_v, gd_out)):
        load.wait()
        store(source, target)
    for copy in stores:
        copy.wait()


def body(src_embed, dst_embed, relation, src_index, dst_index, rel_index, neg_index, edge_count):
    ent, width = src_embed.shape
    rels = relation.shape[0]
    steps = src_index.shape[2]
    nz = lax.axis_size("grp") // NX * ZLO
    half = width // 2
    pieces = -(-rels // (NX * NY * CHUNK))
    rows_mm = -(-rels // 128) * 128
    xrows = NY * CHUNK
    prows = NX * xrows
    tables = [t.reshape(steps, ent) for t in (src_index, dst_index, rel_index, neg_index)]
    vmem = pltpu.VMEM
    dma = pltpu.SemaphoreType.DMA
    block = vmem((ent, width), BF16)
    scratch = [
        vmem((4, ent, width), BF16),
        block,
        block,
        vmem((rels, width), F32),
        vmem((rows_mm, width), F32),
        vmem((2 * width, rows_mm), BF16),
        vmem((width, ent), BF16),
        vmem((4, steps, ent), jnp.int32),
        vmem((4, steps, ent), jnp.int32),
        vmem((1, steps), jnp.int32),
        vmem((1, steps), jnp.int32),
        vmem((ent, 4 * ent), BF16),
        vmem((rows_mm, 4 * ent), BF16),
        vmem((4, width, ent), BF16),
        vmem((4, width, ent), F32),
        vmem((4, width, ent), BF16),
        vmem((4, ent, 1), F32),
        vmem((4, ent, ent), BF16),
        vmem((width, 4 * ent), BF16),
        vmem((width, 4 * ent), BF16),
        vmem((4, ent, width), F32),
        vmem((ent, width), F32),
        vmem((2, pieces * prows, half), F32),
        block, block, block, block, block, block, block, block,
        vmem((pieces, prows, half), F32),
        vmem((pieces, prows, half), BF16),
        vmem((pieces, NX - 1, xrows, half), BF16),
        vmem((pieces, xrows, half), BF16),
        vmem((pieces, NY - 1, CHUNK, half), BF16),
        vmem((pieces, nz, CHUNK, half), F32),
        vmem((pieces, NX, NY, CHUNK, half), BF16),
        dma((5,)),
        dma((3,)),
        dma((3, 2)),
        dma((4, 2)),
        dma((3,)), dma((3,)),
        dma((3,)), dma((3,)),
        dma((2,)), dma((2,)), dma((2,)),
    ] + [dma((pieces,))] * 14
    anywhere = pl.BlockSpec(memory_space=pl.ANY)
    grad = jax.ShapeDtypeStruct((ent, width), F32)
    grad_src, grad_dst, rel_parts = pl.pallas_call(
        functools.partial(kernel, nz, rels, rows_mm, pieces),
        out_shape=(
            grad, grad, jax.ShapeDtypeStruct((2, pieces, NX, NY, CHUNK, half), BF16)
        ),
        in_specs=[anywhere] * 8,
        out_specs=(anywhere,) * 3,
        scratch_shapes=scratch,
        compiler_params=pltpu.CompilerParams(
            collective_id=0, has_side_effects=True, vmem_limit_bytes=56 * 1024 * 1024
        ),
    )(src_embed, dst_embed, relation, *tables, edge_count.reshape(1, steps))
    rel_parts = rel_parts.reshape(2, pieces, prows, half)
    return pl.pallas_call(
        functools.partial(store_kernel, rels),
        out_shape=(grad, grad, jax.ShapeDtypeStruct((rels, width), F32)),
        in_specs=[anywhere] * 3,
        out_specs=(anywhere,) * 3,
        scratch_shapes=[
            vmem(rel_parts.shape, BF16), vmem((rels, width), F32),
            vmem((ent, width), F32), vmem((ent, width), F32),
            dma((2 + 2 * pieces,)), dma((2 + pieces,)),
        ],
        compiler_params=pltpu.CompilerParams(vmem_limit_bytes=56 * 1024 * 1024),
    )(grad_src, grad_dst, rel_parts)


def solution(mesh):
    in_specs = (
        P(("grp", "blk"), None),
        P(("grp", "blk"), None),
        P(),
        P("grp", "blk", None, None),
        P("grp", "blk", None, None),
        P("grp", "blk", None, None),
        P("grp", "blk", None, None),
        P("grp", "blk", None),
    )
    out_specs = (P(("grp", "blk"), None), P(("grp", "blk"), None), P())
    return jax.shard_map(body, mesh=mesh, in_specs=in_specs, out_specs=out_specs, check_vma=False)
```

```python
import functools

import jax
import jax.numpy as jnp
from jax import lax
from jax.experimental import pallas as pl
from jax.experimental.pallas import tpu as pltpu
from jax.sharding import PartitionSpec as P

MESH = pl.DeviceIdType.MESH
F32 = jnp.float32
BF16 = jnp.bfloat16
NX = 4
NY = 8
ZLO = 2
CHUNK = 16
STEP = 128


def nt(a, b):
    return lax.dot_general(a, b, (((1,), (1,)), ((), ())), preferred_element_type=F32)


def nn(a, b):
    return jnp.dot(a, b, preferred_element_type=F32)


def kernel(
    nz, rels, rows_mm, pieces,
    src_hbm, dst_hbm, rel_hbm, si_hbm, di_hbm, ri_hbm, ni_hbm, ec_hbm,
    gs_out, gd_out, rel_out,
    part, src_v, src_far, rel_v, rel_pad, rel_t, src_t, idx, idx_far, ec, ec_far,
    ohs, ohr, sr, rr, qt, weight, pulls, back_v, value, gw, gs, gr,
    gs_send, gs_recv, ga_send, ga_recv, gb_send, gb_recv, gh_send, gh_recv,
    half_recv, xs, x_recv, ys, y_recv, z_all, rel_own,
    in_sem, out_sem, part_send, part_recv, far_send, far_recv,
    g_send, g_recv, h_send, h_recv, h_out, s_send, s_recv,
    xs_send, xs_recv, ys_send, ys_recv, zs_send, zs_recv,
    ya_send, ya_recv, xa_send, xa_recv, ca_send, ca_recv,
):
    ent, width = dst_hbm.shape
    half = width // 2
    yrows = CHUNK
    xrows = NY * yrows
    prows = NX * xrows
    nchip = ZLO * NY
    grp, blk = lax.axis_index("grp"), lax.axis_index("blk")
    core = lax.rem(blk, 2)
    chip = blk // 2
    y = lax.rem(chip, NY)
    z = (grp // NX) * ZLO + chip // NY
    x = lax.rem(grp, NX)
    even = core == 0
    nxt = lax.rem(chip + 1, nchip) * 2 + core
    prv = lax.rem(chip + nchip - 1, nchip) * 2 + core
    sib = (grp, chip * 2 + 1 - core)

    def at_x(i):
        return ((grp // NX) * NX + i, blk)

    def at_y(i):
        return (grp, (chip // NY) * NY * 2 + i * 2 + core)

    def at_z(i):
        return ((i // ZLO) * NX + x, lax.rem(i, ZLO) * NY * 2 + y * 2 + core)

    def ring(place, size):
        steps = sorted(range(1, size), key=lambda k: -min(k, size - k))
        return [(k, lax.rem(place + k, size)) for k in steps]

    x_others, y_others, z_others = ring(x, NX), ring(y, NY), ring(z, nz)

    def remote(source, target, send, recv, device):
        return pltpu.make_async_remote_copy(
            src_ref=source, dst_ref=target, send_sem=send, recv_sem=recv,
            device_id=device, device_id_type=MESH,
        )

    def arrived(buffer, recv):
        pltpu.make_async_copy(buffer, buffer, recv).wait()

    own = [(si_hbm, 0), (di_hbm, 1), (ri_hbm, 2), (ni_hbm, 3)]
    loads = [
        pltpu.make_async_copy(ec_hbm, ec, in_sem.at[3]),
        pltpu.make_async_copy(dst_hbm, part.at[0], in_sem.at[2]),
        pltpu.make_async_copy(src_hbm, src_v, in_sem.at[1]),
        pltpu.make_async_copy(rel_hbm, rel_v, in_sem.at[0]),
    ]
    tables_in = [pltpu.make_async_copy(ref, idx.at[k], in_sem.at[4]) for ref, k in own]
    for load in loads[:2] + tables_in + loads[2:]:
        load.start()
    barrier = pltpu.get_barrier_semaphore()
    greet = [sib, (grp, nxt), (grp, prv)]
    greet += [at_x(i) for _, i in x_others] + [at_y(i) for _, i in y_others]
    greet += [at_z(i) for _, i in z_others]
    for device in greet:
        pl.semaphore_signal(barrier, inc=1, device_id=device, device_id_type=MESH)
    if rows_mm < pieces * prows:
        gr[:, rows_mm:, :] = jnp.zeros((2, pieces * prows - rows_mm, half), F32)
    tail = rels // 8 * 8
    rel_pad[tail:, :] = jnp.zeros((rows_mm - tail, width), F32)

    def tile_of(w):
        if w in (0, 3):
            return w
        return jnp.where(even, 3 - w, w)

    def row_of(k, w):
        row = idx[k, pl.ds(tile_of(w), 1), :]
        if w == 3:
            row = jnp.where(even, idx_far[k, 3:4, :], row)
        return row

    def live_of(w):
        counts = ec[...].astype(F32)
        if w == 3:
            counts = jnp.where(even, ec_far[...].astype(F32), counts)
        place = lax.broadcasted_iota(jnp.int32, counts.shape, 1)
        count = jnp.sum(jnp.where(place == tile_of(w), counts, 0.0), axis=1, keepdims=True)
        slot = lax.broadcasted_iota(jnp.int32, (1, ent), 1).astype(F32)
        return slot < count

    def lanes(w):
        return pl.ds(w * ent, ent)

    def tables(w):
        rows = lax.broadcasted_iota(jnp.int32, (ent, ent), 0)
        ohs[:, lanes(w)] = (rows == jnp.where(live_of(w), row_of(0, w), -1)).astype(BF16)
        chosen = (rows == row_of(3, w)).astype(F32)
        weight[w] = jnp.sum(chosen, axis=1, keepdims=True) * (1.0 / ent)
        rows = lax.broadcasted_iota(jnp.int32, (rows_mm, ent), 0)
        ohr[:, lanes(w)] = (rows == row_of(2, w)).astype(BF16)

    def gather(w):
        picked = nn(src_t[...], ohs[:, lanes(w)])
        both = nn(rel_t[...], ohr[:, lanes(w)])
        scale = both[0:width] + both[width:]
        sr[w] = picked.astype(BF16)
        rr[w] = scale
        qt[w] = (picked * scale).astype(BF16)

    def score(w, slot, h):
        mid = ent // 2
        for low in range(h * mid, (h + 1) * mid, min(STEP, mid)):
            size = min(STEP, mid)
            scores = nn(part[slot, low:low + size, :], qt[w])
            rows = low + lax.broadcasted_iota(jnp.int32, (size, ent), 0)
            decay = jnp.exp(jnp.minimum(-scores, 87.0))
            share = weight[w, low:low + size]
            share = jnp.where(rows == row_of(1, w), share - decay, share)
            inverse = pl.reciprocal(1.0 + decay, approx=True)
            pulls[w, low:low + size] = (inverse * share).astype(BF16)

    def pull_half(w, slot, h):
        return nn(part[slot, halves[h], :].T, pulls[w, halves[h], :])

    def give(w, dquery):
        back_v[:, lanes(w)] = (dquery * rr[w]).astype(BF16)
        value[:, lanes(w)] = (dquery * sr[w].astype(F32)).astype(BF16)

    def finish(w, slot):
        score(w, slot, 0)
        score(w, slot, 1)
        give(w, nn(part[slot].T, pulls[w]))

    def grow(p, first, last):
        low, high = p * prows, min((p + 1) * prows, rows_mm)
        span = pl.ds(first * ent, (last - first) * ent)
        grown = nt(ohr[low:high, span], value[:, span])
        for h in range(2):
            grown_half = grown[:, h * half:(h + 1) * half]
            if first == 0:
                gr[h, low:high, :] = grown_half
            else:
                gr[h, low:high, :] += grown_half

    swaps = [
        remote(
            gr.at[1 - core, pl.ds(p * prows, prows)], half_recv.at[p],
            s_send.at[p], s_recv.at[p], sib,
        )
        for p in range(pieces)
    ]

    arrived(idx, in_sem.at[4])
    loads[0].wait()
    for w in range(3):
        tables(w)

    pl.semaphore_wait(barrier, len(greet))

    direct = 2 - core
    other = 1 + core
    halves = [pl.ds(0, ent // 2), pl.ds(ent // 2, ent // 2)]

    def send_part(source, slot, h, send, device):
        return remote(
            source.at[halves[h]], part.at[slot, halves[h]], part_send.at[send, h],
            part_recv.at[slot, h], device,
        )

    def arrived_part(slot, h):
        arrived(part.at[slot, halves[h]], part_recv.at[slot, h])

    send_next = [send_part(part.at[0], direct, h, 0, (grp, nxt)) for h in range(2)]
    send_sib = [send_part(part.at[0], 3, h, 1, sib) for h in range(2)]
    forward = [send_part(part.at[direct], direct, h, 2, sib) for h in range(2)]
    loads[1].wait()
    for copy in send_next:
        copy.start()
    far = [remote(src_hbm, src_far, far_send.at[0], far_recv.at[0], (grp, prv))]
    far += [remote(ec_hbm, ec_far, far_send.at[1], far_recv.at[1], (grp, prv))]
    far += [
        remote(ref, idx_far.at[k], far_send.at[2], far_recv.at[2], (grp, prv))
        for ref, k in own
    ]

    @pl.when(even)
    def _():
        for copy in send_sib + far:
            copy.start()

    for load in loads[2:]:
        load.wait()
    rel_pad[0:rels, :] = rel_v[...]
    turned = rel_pad[...].T
    high = turned.astype(BF16)
    rel_t[0:width, :] = high
    rel_t[width:, :] = (turned - high.astype(F32)).astype(BF16)
    src_t[...] = src_v[...].T

    gather(0)
    gather(1)
    finish(0, 0)
    gather(2)
    for p in range(pieces):
        grow(p, 0, 1)

    @pl.when(even)
    def _():
        arrived(idx_far, far_recv.at[2])
        arrived(ec_far, far_recv.at[1])
        arrived(src_far, far_recv.at[0])
        src_t[...] = src_far[...].T

    tables(3)
    gather(3)

    for h in range(2):
        arrived_part(direct, h)
        forward[h].start()

    @pl.when(core == 1)
    def _():
        arrived_part(3, 0)
        arrived_part(3, 1)

    finish(1, 2 + core)
    for p in range(pieces):
        grow(p, 1, 2)
    arrived_part(other, 0)
    score(2, 1, 0)
    score(3, other, 0)
    first = [pull_half(2, 1, 0), pull_half(3, other, 0)]
    arrived_part(other, 1)
    score(2, 1, 1)
    score(3, other, 1)
    give(2, first[0] + pull_half(2, 1, 1))
    give(3, first[1] + pull_half(3, other, 1))
    for p in range(pieces):
        grow(p, 2, 4)
        swaps[p].start()

    sent = send_next + forward + swaps

    def rows_at(i, size):
        return pl.ds(pl.multiple_of(i * size, size), size)

    for p in range(pieces):
        arrived(half_recv.at[p], s_recv.at[p])
        xs[p] = (gr[core, p * prows:(p + 1) * prows, :] + half_recv[p]).astype(BF16)
        for k, i in x_others:
            remote(
                xs.at[p, rows_at(i, xrows)], x_recv.at[p, k - 1], xs_send.at[p], xs_recv.at[p], at_x(i)
            ).start()

    last = nt(ohs[:, lanes(3)], back_v[:, lanes(3)])
    gs_send[...] = last.astype(BF16)
    src_copy = remote(gs_send, gs_recv, g_send.at[2], g_recv.at[2], (grp, nxt))

    @pl.when(even)
    def _():
        src_copy.start()

    for w in range(4):
        gw[w] = nt(pulls[w], qt[w])
    ga_send[...] = (gw[3] + jnp.where(even, gw[2], 0.0)).astype(BF16)
    pair_copy = remote(ga_send, ga_recv, g_send.at[1], g_recv.at[1], sib)
    pair_copy.start()
    sent.append(pair_copy)
    gb_send[...] = gw[1].astype(BF16)
    home_copy = remote(gb_send, gb_recv, g_send.at[0], g_recv.at[0], sib)

    @pl.when(core == 1)
    def _():
        home_copy.start()

    own_slots = pl.ds(0, 3 * ent)
    gs[...] = nt(ohs[:, own_slots], back_v[:, own_slots])

    @pl.when(core == 1)
    def _():
        gs[...] += last

    for p in range(pieces):
        total = xs[p, rows_at(x, xrows), :].astype(F32)
        arrived(x_recv.at[p], xs_recv.at[p])
        for k in range(NX - 1):
            total = total + x_recv[p, k].astype(F32)
        ys[p] = total.astype(BF16)
        for k, i in y_others:
            remote(
                ys.at[p, rows_at(i, yrows)], y_recv.at[p, k - 1], ys_send.at[p], ys_recv.at[p], at_y(i)
            ).start()

    arrived(ga_recv, g_recv.at[1])
    gh_send[...] = (gw[1 + core] + ga_recv[...].astype(F32)).astype(BF16)

    for p in range(pieces):
        total = ys[p, rows_at(y, yrows), :].astype(F32)
        arrived(y_recv.at[p], ys_recv.at[p])
        for k in range(NY - 1):
            total = total + y_recv[p, k].astype(F32)
        z_all[p, 0] = total
        for k, i in z_others:
            remote(
                z_all.at[p, 0], z_all.at[p, k], zs_send.at[p], zs_recv.at[p], at_z(i)
            ).start()

    @pl.when(even)
    def _():
        arrived(gs_recv, g_recv.at[2])
        gs[...] += gs_recv[...].astype(F32)
        arrived(gb_recv, g_recv.at[0])
        gw[0] = gw[0] + gb_recv[...].astype(F32)

    gs_copy = pltpu.make_async_copy(gs, gs_out, out_sem.at[0])
    gs_copy.start()
    for p in range(pieces):
        arrived(z_all.at[p, pl.ds(1, nz - 1)], zs_recv.at[p])
        total = z_all[p, z]
        for i in range(1, nz):
            total = total + z_all[p, lax.rem(z + nz - i, nz)]
        piece = rel_own.at[p, x, y]
        piece[...] = total.astype(BF16)
        for _, i in y_others:
            remote(piece, piece, ya_send.at[p], ya_recv.at[p], at_y(i)).start()

    for p in range(pieces):
        arrived(rel_own.at[p, x, pl.ds(0, NY - 1)], ya_recv.at[p])
        piece = rel_own.at[p, x]
        for _, i in x_others:
            remote(piece, piece, xa_send.at[p], xa_recv.at[p], at_x(i)).start()
    homeward = [
        remote(gh_send.at[part_rows], gh_recv.at[part_rows], h_send.at[h], h_recv.at[h], (grp, prv))
        for h, part_rows in enumerate(halves)
    ]
    for copy in homeward:
        copy.start()
    sent += homeward
    for p in range(pieces):
        arrived(rel_own.at[p, pl.ds(0, NX - 1)], xa_recv.at[p])
        remote(rel_own.at[p], rel_out.at[core, p], ca_send.at[p], ca_recv.at[p], sib).start()
        pltpu.make_async_copy(rel_own.at[p], rel_out.at[core, p], out_sem.at[2]).start()

    gd_copies = []
    for h, part_rows in enumerate(halves):
        arrived(gh_recv.at[part_rows], h_recv.at[h])
        gw[0, part_rows, :] = gw[0, part_rows, :] + gh_recv[part_rows, :].astype(F32)
        gd_copies.append(
            pltpu.make_async_copy(gw.at[0, part_rows], gd_out.at[part_rows], h_out.at[h])
        )
        gd_copies[h].start()

    for copy in sent:
        copy.wait_send()

    @pl.when(even)
    def _():
        for copy in send_sib + far[:2]:
            copy.wait_send()
        arrived(idx, far_send.at[2])
        src_copy.wait_send()

    @pl.when(core == 1)
    def _():
        home_copy.wait_send()

    for p in range(pieces):
        arrived(x_recv.at[p], xs_send.at[p])
        arrived(y_recv.at[p], ys_send.at[p])
        arrived(z_all.at[p, pl.ds(1, nz - 1)], zs_send.at[p])
        arrived(rel_own.at[p, x, pl.ds(0, NY - 1)], ya_send.at[p])
        arrived(rel_own.at[p, pl.ds(0, NX - 1)], xa_send.at[p])
        arrived(rel_own.at[p], ca_send.at[p])
    gs_copy.wait()
    for copy in gd_copies:
        copy.wait()
    arrived(rel_own, out_sem.at[2])
    for p in range(pieces):
        arrived(rel_out.at[1 - core, p], ca_recv.at[p])


def store_kernel(
    rels, gs_in, gd_in, rel_in, gs_out, gd_out, rel_out, rel_b, rel_f, gs_v, gd_v, in_sem, out_sem
):
    pieces, rows, half = rel_b.shape[1:]
    spans = [(p * rows, min((p + 1) * rows, rels)) for p in range(pieces)]
    loads = [
        pltpu.make_async_copy(rel_in.at[h, p], rel_b.at[h, p], in_sem.at[2 + 2 * p + h])
        for p in range(pieces) for h in range(2)
    ] + [
        pltpu.make_async_copy(gs_in, gs_v, in_sem.at[0]),
        pltpu.make_async_copy(gd_in, gd_v, in_sem.at[1]),
    ]
    for load in loads:
        load.start()
    stores = []

    def store(source, target):
        stores.append(pltpu.make_async_copy(source, target, out_sem.at[len(stores)]))
        stores[-1].start()

    for p, (low, high) in enumerate(spans):
        for h in range(2):
            loads[2 * p + h].wait()
            rel_f[low:high, h * half:(h + 1) * half] = rel_b[h, p, 0:high - low, :].astype(F32)
        store(rel_f.at[low:high], rel_out.at[low:high])
    for load, source, target in ((loads[-2], gs_v, gs_out), (loads[-1], gd_v, gd_out)):
        load.wait()
        store(source, target)
    for copy in stores:
        copy.wait()


def body(src_embed, dst_embed, relation, src_index, dst_index, rel_index, neg_index, edge_count):
    ent, width = src_embed.shape
    rels = relation.shape[0]
    steps = src_index.shape[2]
    nz = lax.axis_size("grp") // NX * ZLO
    half = width // 2
    pieces = -(-rels // (NX * NY * CHUNK))
    rows_mm = -(-rels // 128) * 128
    xrows = NY * CHUNK
    prows = NX * xrows
    tables = [t.reshape(steps, ent) for t in (src_index, dst_index, rel_index, neg_index)]
    vmem = pltpu.VMEM
    dma = pltpu.SemaphoreType.DMA
    block = vmem((ent, width), BF16)
    scratch = [
        vmem((4, ent, width), BF16),
        block,
        block,
        vmem((rels, width), F32),
        vmem((rows_mm, width), F32),
        vmem((2 * width, rows_mm), BF16),
        vmem((width, ent), BF16),
        vmem((4, steps, ent), jnp.int32),
        vmem((4, steps, ent), jnp.int32),
        vmem((1, steps), jnp.int32),
        vmem((1, steps), jnp.int32),
        vmem((ent, 4 * ent), BF16),
        vmem((rows_mm, 4 * ent), BF16),
        vmem((4, width, ent), BF16),
        vmem((4, width, ent), F32),
        vmem((4, width, ent), BF16),
        vmem((4, ent, 1), F32),
        vmem((4, ent, ent), BF16),
        vmem((width, 4 * ent), BF16),
        vmem((width, 4 * ent), BF16),
        vmem((4, ent, width), F32),
        vmem((ent, width), F32),
        vmem((2, pieces * prows, half), F32),
        block, block, block, block, block, block, block, block,
        vmem((pieces, prows, half), F32),
        vmem((pieces, prows, half), BF16),
        vmem((pieces, NX - 1, xrows, half), BF16),
        vmem((pieces, xrows, half), BF16),
        vmem((pieces, NY - 1, CHUNK, half), BF16),
        vmem((pieces, nz, CHUNK, half), F32),
        vmem((pieces, NX, NY, CHUNK, half), BF16),
        dma((5,)),
        dma((3,)),
        dma((3, 2)),
        dma((4, 2)),
        dma((3,)), dma((3,)),
        dma((3,)), dma((3,)),
        dma((2,)), dma((2,)), dma((2,)),
    ] + [dma((pieces,))] * 14
    anywhere = pl.BlockSpec(memory_space=pl.ANY)
    grad = jax.ShapeDtypeStruct((ent, width), F32)
    grad_src, grad_dst, rel_parts = pl.pallas_call(
        functools.partial(kernel, nz, rels, rows_mm, pieces),
        out_shape=(
            grad, grad, jax.ShapeDtypeStruct((2, pieces, NX, NY, CHUNK, half), BF16)
        ),
        in_specs=[anywhere] * 8,
        out_specs=(anywhere,) * 3,
        scratch_shapes=scratch,
        compiler_params=pltpu.CompilerParams(
            collective_id=0, has_side_effects=True, vmem_limit_bytes=56 * 1024 * 1024
        ),
    )(src_embed, dst_embed, relation, *tables, edge_count.reshape(1, steps))
    rel_parts = rel_parts.reshape(2, pieces, prows, half)
    return pl.pallas_call(
        functools.partial(store_kernel, rels),
        out_shape=(grad, grad, jax.ShapeDtypeStruct((rels, width), F32)),
        in_specs=[anywhere] * 3,
        out_specs=(anywhere,) * 3,
        scratch_shapes=[
            vmem(rel_parts.shape, BF16), vmem((rels, width), F32),
            vmem((ent, width), F32), vmem((ent, width), F32),
            dma((2 + 2 * pieces,)), dma((2 + pieces,)),
        ],
        compiler_params=pltpu.CompilerParams(vmem_limit_bytes=56 * 1024 * 1024),
    )(grad_src, grad_dst, rel_parts)


def solution(mesh):
    in_specs = (
        P(("grp", "blk"), None),
        P(("grp", "blk"), None),
        P(),
        P("grp", "blk", None, None),
        P("grp", "blk", None, None),
        P("grp", "blk", None, None),
        P("grp", "blk", None, None),
        P("grp", "blk", None),
    )
    out_specs = (P(("grp", "blk"), None), P(("grp", "blk"), None), P())
    return jax.shard_map(body, mesh=mesh, in_specs=in_specs, out_specs=out_specs, check_vma=False)
```
